512 devices in a mesh: grp: 16 (over z_lo, core), lane: 32 (over z_hi, y, x).
Axes of the slice: x: 4, y: 4, z: 16 (z_hi: 2, z_lo: 8; z = z_hi * 8 + z_lo), core: 2. Of those that a mesh axis runs over, the one named last changes fastest.
Arguments:
- estimate: float32 [16, 1024, 1024], P('grp', 'lane'), may hold values from 0.5 to 2
- view_lines: float32 [4, 16384, 1024], P(None, ('grp', 'lane')), may hold values from 0.25 to 4
- line_owner: int32 [4, 16384, 1], P(None, ('grp', 'lane')), may hold values from 0 to 15; in each aligned block of 32 rows (0 to 31, 32 to 63, ..., all dimensions but the last counted through in order) at most 4 rows name the same one
- line_target: int32 [4, 16384], P(None, ('grp', 'lane')), may hold values from 0 to 31
- view_shift: int32 [4], replicated, may hold values from -16 to 16
- psf_x: float32 [4, 3], replicated, may hold values from 0.3 to 1
- psf_yz: float32 [4, 2, 41], replicated, may hold values from 0.001 to 1.5, as said below
Outputs:
- deconvolved: float32 [16, 1024, 1024], P('grp', 'lane')
The draws below stay inside these ranges and needn't reach their ends.
Inputs may be any that keep to these rules, and one draw needn't show every extreme that they name: `line_owner`: for each view, among the 32 lines of one device no owner index appears more than 4 times, and some owner appears exactly 4 times in some of these blocks. `psf_yz`: positive tap weights.
All inputs are finite; a program needn't handle non-finite values.
Results may differ from the reference program's by a relative error of at most 0.0001.
Values sent between devices are 32-bit elements; how exact they have to be, the bound alone decides.
A program may use at most 128 MiB of HBM per device.

```python
import math
import jax
import jax.numpy as jnp
import numpy as np
from jax import lax

VIEWS = 4
KT = 41
KX = 3
ITERS = 2
SHIFT = 16
XD = 1
ZD = 32
SRC_DEV = 32
X = 16
Y = 1024
Z = 1024
SRC = 16384
CAP = 4
LINES = 32
N_GRP = 16
N_LANE = 32


def draw_psf_yz(key, part):
    key_width, key_rough = jax.random.split(key)
    spread_width = jax.random.uniform(key_width, (VIEWS, 2, 1), jnp.float32, 1.5, 5.0)
    position = jnp.arange(KT, dtype=jnp.float32) - (KT - 1) / 2.0
    scaled = position / spread_width
    profile = jnp.exp(-0.5 * scaled * scaled) + 0.002
    roughness = jnp.exp(jax.random.uniform(key_rough, (VIEWS, 2, KT), jnp.float32, -0.35, 0.35))
    return (profile * roughness).astype(jnp.float32)


def set_ends(values, rng, low, top_value):
    dims = values.shape
    spot = [jax.random.randint(jax.random.fold_in(rng, axis), (), 0, dims[axis]) for axis in range(len(dims))]
    values = values.at[tuple(spot)].set(low)
    longest = dims.index(max(dims))
    spot[longest] = (spot[longest] + 1) % dims[longest]
    return values.at[tuple(spot)].set(top_value)


def block_levels(stream_key, shape, cuts, low, high):
    factor_of, own = 1.0, jax.random.fold_in(stream_key, 6)
    for dim, blocks in cuts:
        steps = jnp.exp(jax.random.uniform(jax.random.fold_in(own, dim), (blocks,), jnp.float32, low / len(cuts), high / len(cuts)))
        factor_of = factor_of * jnp.repeat(steps, shape[dim] // blocks).reshape([-1 if axis == dim else 1 for axis in range(len(shape))])
    return factor_of


def shared_out(key, own, number, rows, amount, top, limit, skew):
    ranking = jax.random.permutation(key, amount)
    crowded, ordinary = portions_of(amount, rows * top, limit, skew, True), portions_of(amount, rows * top, limit, skew, False)
    places = jnp.arange(amount)

    def named(tallies, offset_by):
        used = int((tallies > 0).sum())
        fixed = max(1, used // 4)
        moved = fixed + (places - fixed + offset_by * (used - fixed)) % max(1, amount - fixed)
        return jnp.zeros((amount,), jnp.int32).at[ranking[jnp.where(places < fixed, places, moved)]].set(jnp.asarray(tallies, jnp.int32))

    tallies = jnp.where(number % 4 == 0, named(crowded, number // 4), named(ordinary, number - number // 4 - 1))
    mixed = jax.random.permutation(jax.random.fold_in(own, 3), amount)
    source_of, receiver = mixed[0:amount // 2 * 2:2], mixed[1:amount // 2 * 2:2]
    margin = jnp.minimum(tallies[source_of] - 1, limit - tallies[receiver]) // 2
    margin = jnp.where((source_of == ranking[0]) | (receiver == ranking[0]) | (tallies[receiver] == 0), 0, jnp.maximum(margin, 0))
    moved = jax.random.randint(jax.random.fold_in(own, 4), (amount // 2,), 0, 1 << 20) % (margin + 1)
    tallies = tallies.at[source_of].add(-moved).at[receiver].add(moved)
    members = jnp.searchsorted(jnp.cumsum(tallies), jnp.arange(rows * top), side="right").astype(jnp.int32)
    table = members.reshape(top, rows).T
    table = table[jax.random.permutation(jax.random.fold_in(own, 1), rows)]
    offset_by = jax.random.randint(jax.random.fold_in(own, 2), (rows, 1), 0, top)
    return jnp.take_along_axis(table, (jnp.arange(top)[None, :] + offset_by) % top, axis=1)


def portions_of(amount, total, bound, skew, full):
    loads = [(1 << 20) // math.isqrt(standing ** skew) + 1 for standing in range(1, amount + 1)]
    largest = bound if full else min(bound, max(-(-total // amount), total * loads[0] // sum(loads)))
    least = 1 if total - largest >= amount - 1 else 0
    counts, rest = [largest] + [least] * (amount - 1), total - largest - least * (amount - 1)
    while rest > 0:
        free = [i for i in range(1, amount) if counts[i] < largest] or [i for i in range(1, amount) if counts[i] < bound]
        mass, left = sum([loads[i] for i in free]), rest
        for i in free:
            addition = min(bound - counts[i], max(1, left * loads[i] // mass), rest)
            counts[i] = counts[i] + addition
            rest = rest - addition
    return np.array(counts)


def setup_inputs(seed: int = 0) -> dict:
    key_of = jax.random.split(jax.random.key(seed), 8)
    estimate = jnp.clip(jnp.exp(math.log(2.0) - 1.3862944 * jax.random.uniform(key_of[0], (X, Z, Y), jnp.float32) ** block_levels(key_of[0], (X, Z, Y), ((0, 16), (1, 32)), -0.2, 0.2)), 0.5, 2.0)
    view_lines = jnp.clip(jnp.exp(math.log(4.0) - 2.7725887 * jax.random.uniform(key_of[1], (VIEWS, SRC, Y), jnp.float32) ** block_levels(key_of[1], (VIEWS, SRC, Y), ((1, 512),), -0.2, 0.2)), 0.25, 4.0)
    line_owner_keys = jax.random.split(jax.random.fold_in(key_of[2], 1), VIEWS * SRC // SRC_DEV)
    line_owner_turns = jax.random.permutation(jax.random.fold_in(key_of[2], 3), VIEWS * SRC // SRC_DEV)
    line_owner = jax.vmap(lambda own, number: shared_out(jax.random.fold_in(key_of[2], 2), own, number, SRC_DEV, N_GRP, 1, CAP, 1))(line_owner_keys, line_owner_turns).reshape((VIEWS, SRC, 1))
    line_target = set_ends(jax.random.randint(key_of[3], (VIEWS, SRC), 0, LINES), jax.random.fold_in(key_of[3], 1), 0, LINES - 1).astype(jnp.int32)
    view_shift = set_ends(jax.random.randint(key_of[4], (VIEWS,), 0 - SHIFT, SHIFT + 1), jax.random.fold_in(key_of[4], 1), 0 - SHIFT, SHIFT).astype(jnp.int32)
    psf_x = jnp.clip(jnp.exp(jax.random.uniform(key_of[5], (VIEWS, KX), jnp.float32, math.log(0.3), math.log(1.0))), 0.3, 1.0)
    psf_yz = draw_psf_yz(jax.random.fold_in(key_of[7], 71), 0)
    return dict(estimate=estimate, view_lines=view_lines, line_owner=line_owner, line_target=line_target, view_shift=view_shift, psf_x=psf_x, psf_yz=psf_yz)


def convolve(volume, kernel, axis_at, adjoint):
    extent = (kernel.shape[0] - 1) // 2
    moved = jnp.moveaxis(volume, axis_at, -1)
    length = moved.shape[-1]
    lined = moved.reshape(-1, 1, length)
    weights = kernel if adjoint else kernel[::-1]
    result = lax.conv_general_dilated(lined, weights.reshape(1, 1, -1), (1,), [(extent, extent)], precision=lax.Precision.HIGHEST)
    return jnp.moveaxis(result.reshape(moved.shape), -1, axis_at)


def reference(estimate, view_lines, line_owner, line_target, view_shift, psf_x, psf_yz):
    plane_count, depth_count, width_y = estimate.shape
    taps_x = psf_x / jnp.sum(psf_x, axis=1, keepdims=True)
    taps_yz = psf_yz / jnp.sum(psf_yz, axis=2, keepdims=True)
    padded = jnp.pad(view_lines, ((0, 0), (0, 0), (SHIFT, SHIFT)))
    source = jnp.arange(view_lines.shape[1], dtype=jnp.int32)
    lane_of = (source // SRC_DEV) % N_LANE
    observed_views = []
    for view_at in range(VIEWS):
        start = (SHIFT - view_shift[view_at]).astype(jnp.int32)
        shifted = lax.dynamic_slice_in_dim(padded[view_at], start, width_y, 1)
        target = line_target[view_at].astype(jnp.int32)
        plane_at = line_owner[view_at, :, 0].astype(jnp.int32) * XD + target // ZD
        depth_at = lane_of * ZD + target % ZD
        empty = jnp.zeros((plane_count, depth_count, width_y), jnp.float32)
        observed_views.append(empty.at[plane_at, depth_at].add(shifted))
    current = estimate
    for sweep_at in range(ITERS):
        correction = jnp.zeros_like(current)
        for view_at in range(VIEWS):
            blurred = convolve(current, taps_x[view_at], 0, False)
            blurred = convolve(blurred, taps_yz[view_at, 0], 2, False)
            blurred = convolve(blurred, taps_yz[view_at, 1], 1, False)
            quotient = observed_views[view_at] / blurred
            returned = convolve(quotient, taps_yz[view_at, 1], 1, True)
            returned = convolve(returned, taps_yz[view_at, 0], 2, True)
            returned = convolve(returned, taps_x[view_at], 0, True)
            correction = correction + returned
        current = current * correction / VIEWS
    return current
```

```python
import functools

import jax
import jax.numpy as jnp
from jax import lax
from jax.experimental import pallas as pl
from jax.experimental.pallas import tpu as pltpu
from jax.sharding import PartitionSpec as P

ITERS = 2
HALO = 24
MESH = pl.DeviceIdType.MESH
F32, BF16 = jnp.float32, jnp.bfloat16


def halves(x):
    high = x.astype(BF16)
    return high, (x - high.astype(F32)).astype(BF16)


def dot(a, b):
    return jnp.dot(a, b, preferred_element_type=F32)


def iota(shape, dim):
    return lax.broadcasted_iota(jnp.int32, shape, dim)


def total_of(ref, *at, size):
    summed = ref[(*at, 0)]
    for k in range(1, size):
        summed = summed + ref[(*at, k)]
    return summed


def along_y(x, taps):
    rows, width = x.shape
    blocks = width // 128
    padded = pltpu.roll(jnp.concatenate([x, jnp.zeros((rows, 128), F32)], axis=1), 64, 1)
    high, low = halves(padded)
    windows = [part[:, 128 * b : 128 * b + 256] for part in (high, low) for b in range(blocks)]
    r = dot(jnp.concatenate(windows, axis=0), taps)
    n = blocks * rows
    summed = r[:n, :128] + (r[:n, 128:] + r[n:, :128])
    return jnp.concatenate([summed[rows * b : rows * (b + 1)] for b in range(blocks)], axis=1)


def kernel(groups, lanes, views, cap, est, lines, codes, shift, psf_x, psf_yz, out,
           outgoing, arrived, meta_out, meta_in, cur, part, part_in, edge, edge_in,
           m_fwd, m_adj, m_adj_low, t_fwd, t_adj, observed, blurred, spread,
           send_sem, recv_sem, a2a_send, a2a_recv, meta_send, meta_recv):
    p, l = lax.axis_index("grp"), lax.axis_index("lane")
    depth, width = est.shape
    taps = psf_yz.shape[2]
    reach = (taps - 1) // 2
    slots = views * cap
    span = depth + 2 * HALO
    all_rows = views * depth
    chunk = min(256, width)
    has = {"before": p > 0, "after": p < groups - 1, "up": l > 0, "down": l < lanes - 1}
    where = {
        "before": (jnp.maximum(p - 1, 0), l),
        "after": (jnp.minimum(p + 1, groups - 1), l),
        "up": (p, jnp.maximum(l - 1, 0)),
        "down": (p, jnp.minimum(l + 1, lanes - 1)),
    }
    opposite = {"before": "after", "after": "before", "up": "down", "down": "up"}
    counter = [0]

    class Copy:
        def __init__(self, side, src, dst):
            at = counter[0]
            counter[0] += 1
            self.to, self.since = has[side], has[opposite[side]]
            self.copy = pltpu.make_async_remote_copy(
                src_ref=src, dst_ref=dst, send_sem=send_sem.at[at], recv_sem=recv_sem.at[at],
                device_id=where[side], device_id_type=MESH,
            )
            pl.when(self.to)(self.copy.start)

        def arrive(self):
            pl.when(self.since)(self.copy.wait_recv)

        def leave(self):
            pl.when(self.to)(self.copy.wait_send)

    for it in range(ITERS):
        cur[it, 3 * span :] = jnp.zeros((cur.shape[1] - 3 * span, width), F32)

    @pl.when(p == 0)
    def _():
        for it in range(ITERS):
            cur[it, 0:span] = jnp.zeros((span, width), F32)
            part_in[it, 0] = jnp.zeros((span, width), F32)

    @pl.when(p == groups - 1)
    def _():
        for it in range(ITERS):
            cur[it, 2 * span : 3 * span] = jnp.zeros((span, width), F32)
            part_in[it, 1] = jnp.zeros((span, width), F32)

    @pl.when(l == 0)
    def _():
        for it in range(ITERS):
            for plane in range(3):
                cur[it, plane * span : plane * span + HALO] = jnp.zeros((HALO, width), F32)
            edge_in[it, 0] = jnp.zeros((HALO, width), F32)

    @pl.when(l == lanes - 1)
    def _():
        for it in range(ITERS):
            for plane in range(3):
                cur[it, (plane + 1) * span - HALO : (plane + 1) * span] = jnp.zeros((HALO, width), F32)
            edge_in[it, 1] = jnp.zeros((HALO, width), F32)

    barrier = pltpu.get_barrier_semaphore()
    for k in range(1, groups):
        pl.semaphore_signal(barrier, inc=1, device_id=(lax.rem(p + k, groups), l), device_id_type=MESH)
    for side in ("up", "down"):

        @pl.when(has[side])
        def _(side=side):
            pl.semaphore_signal(barrier, inc=1, device_id=where[side], device_id_type=MESH)

    own = pl.ds(span + HALO, depth)
    cur[0, own] = est[...]

    n_lines = codes.shape[1]
    per_view = n_lines // views
    code = codes[...]
    owner, landing = code // depth, code % depth
    line_at = iota((1, n_lines), 1)
    view = line_at // per_view
    key = view * groups + owner
    wide = jnp.broadcast_to(key, (n_lines, n_lines))
    earlier = iota((n_lines, n_lines), 0) < iota((n_lines, n_lines), 1)
    same = jnp.where((wide == wide.T) & earlier, 1.0, 0.0)
    rank = jnp.sum(same, axis=0, keepdims=True).astype(jnp.int32)
    in_block = view * cap + rank
    picks = jnp.where(iota((groups * slots, n_lines), 0) == owner * slots + in_block, 1.0, 0.0).astype(BF16)
    named = jnp.where(iota((groups, n_lines), 0) == owner, view * depth + landing + 1, 0)
    place = jnp.where(iota((groups * slots, n_lines), 0) == p * slots + in_block, 1.0, 0.0).astype(BF16)
    meta = lax.dot_general(
        named.astype(F32).astype(BF16), place, (((1,), (1,)), ((), ())), preferred_element_type=F32
    )
    for g in range(groups):
        meta_out[g] = meta[g : g + 1]
    picks2 = jnp.concatenate([picks, picks], axis=1)
    for at in range(0, width, chunk):
        high, low = halves(lines[:, at : at + chunk])
        packed = dot(picks2, jnp.concatenate([high, low], axis=0))
        outgoing[:, :, at : at + chunk] = packed.reshape(groups, slots, chunk)

    pl.semaphore_wait(
        barrier, groups - 1 + jnp.where(has["up"], 1, 0) + jnp.where(has["down"], 1, 0)
    )

    def widen_start(it):
        now = cur.at[it]
        lo, hi = span, 2 * span
        ups = [
            Copy("up", now.at[lo + HALO : lo + 2 * HALO], now.at[hi - HALO : hi]),
            Copy("down", now.at[hi - 2 * HALO : hi - HALO], now.at[lo : lo + HALO]),
        ]
        own_rows = now.at[lo + HALO : hi - HALO]
        mids = [
            Copy("before", own_rows, now.at[2 * span + HALO : 3 * span - HALO]),
            Copy("after", own_rows, now.at[HALO : span - HALO]),
        ]
        return ups, mids

    def widen_finish(it, ups, mids):
        now = cur.at[it]
        for c, at in ((ups[1], 0), (ups[0], span - HALO)):
            c.arrive()
            got = now.at[span + at : span + at + HALO]
            mids.append(Copy("before", got, now.at[2 * span + at : 2 * span + at + HALO]))
            mids.append(Copy("after", got, now.at[at : at + HALO]))
        for c in mids:
            c.arrive()
        for c in ups + mids:
            c.leave()

    ups, mids = widen_start(0)
    routes = []
    for k in sorted(range(1, groups), key=lambda k: -min(k, groups - k)):
        to = (lax.rem(p + k, groups), l)
        for src, dst, sent, got in (
            (meta_out.at[to[0]], meta_in.at[p], meta_send, meta_recv),
            (outgoing.at[to[0]], arrived.at[p], a2a_send, a2a_recv),
        ):
            c = pltpu.make_async_remote_copy(
                src_ref=src, dst_ref=dst, send_sem=sent.at[k], recv_sem=got.at[k],
                device_id=to, device_id_type=MESH,
            )
            c.start()
            routes.append(c)
    arrived[p] = outgoing[p]
    meta_in[p] = meta_out[p]

    columns = m_fwd.shape[1]
    column = iota((depth, columns), 1)
    plane = jnp.where(column < span, 0, jnp.where(column < 2 * span, 1, 2))
    tap_at = iota((depth, columns), 0) + (reach + HALO) - (column - plane * span)
    tap_at = jnp.where(column < 3 * span, tap_at, -1)
    blocks = []
    for v in range(views):
        acc = jnp.zeros((depth, columns), F32)
        for t in range(taps):
            acc = jnp.where(tap_at == t, psf_yz[v, 1, t], acc)
        across = jnp.where(plane == 0, psf_x[v, 2], jnp.where(plane == 1, psf_x[v, 1], psf_x[v, 0]))
        norm = jnp.full((1, columns), total_of(psf_yz, v, 1, size=taps)) * jnp.full(
            (1, columns), total_of(psf_x, v, size=3)
        )
        blocks.append(acc * across / norm)
    matrix = jnp.concatenate(blocks, axis=0)
    high, low = halves(matrix)
    m_fwd[0:all_rows] = high
    m_fwd[all_rows:] = low
    high, low = halves(matrix.T)
    m_adj[:, 0:all_rows] = high
    m_adj[:, all_rows:] = high
    m_adj_low[...] = low

    rows = 32

    def band(step, carry):
        i = iota((rows, 128), 0) + step * rows
        j = iota((rows, 128), 1)
        for v in range(views):
            norm = jnp.full((1, 128), total_of(psf_yz, v, 0, size=taps))
            for ref, at in ((t_fwd, j - i + (64 + reach + shift[v])), (t_adj, i - j + (reach - 64 + shift[v]))):
                acc = jnp.zeros((rows, 128), F32)
                for t in range(taps):
                    acc = jnp.where(at == t, psf_yz[v, 0, t], acc)
                high, low = halves(acc / norm)
                ref[v, pl.ds(pl.multiple_of(step * rows, rows), rows), 0:128] = high
                ref[v, pl.ds(pl.multiple_of(step * rows, rows), rows), 128:256] = low
        return carry

    lax.fori_loop(0, 256 // rows, band, 0)

    def blur(it):
        for at in range(0, width, chunk):
            high, low = halves(cur[it, :, at : at + chunk])
            r = dot(m_fwd[...], high)
            spread[:, at : at + chunk] = r[:all_rows] + (r[all_rows:] + dot(m_fwd[0:all_rows], low))
        for v in range(views):
            blurred[v * depth : (v + 1) * depth] = along_y(spread[v * depth : (v + 1) * depth], t_fwd[v])

    widen_finish(0, ups, mids)
    blur(0)

    for c in routes:
        c.wait()
    marks = jnp.sum(meta_in[...], axis=0)
    lands = jnp.where(iota((all_rows, groups * slots), 0) + 1 == marks.astype(jnp.int32), 1.0, 0.0).astype(BF16)
    for at in range(0, width, chunk):
        high, low = halves(arrived[:, :, at : at + chunk].reshape(groups * slots, chunk))
        observed[:, at : at + chunk] = dot(lands, high) + dot(lands, low)

    for it in range(ITERS):
        if it > 0:
            widen_finish(it, *widen_start(it))
            blur(it)
        y = iota((depth, width), 1)
        for v in range(views):
            at = pl.ds(v * depth, depth)
            seen = y + shift[v]
            quotient = jnp.where((seen >= 0) & (seen < width), observed[at] / blurred[at], 0.0)
            spread[at] = along_y(quotient, t_adj[v])
        for at in range(0, width, chunk):
            high, low = halves(spread[:, at : at + chunk])
            r = dot(m_adj[...], jnp.concatenate([high, low], axis=0)) + dot(m_adj_low[...], high)
            part[it, :, at : at + chunk] = r
        mine, theirs = part.at[it], part_in.at[it]
        shares = []
        for rows_at in ((0, HALO), (span - HALO, span), (HALO, span - HALO)):
            a, b = rows_at
            shares.append([
                Copy("before", mine.at[a:b], theirs.at[1, a:b]),
                Copy("after", mine.at[2 * span + a : 2 * span + b], theirs.at[0, a:b]),
            ])
        edges = []
        for n, (side, a) in enumerate((("up", 0), ("down", span - HALO))):
            for c in shares[n]:
                c.arrive()
            rows_at = pl.ds(a, HALO)
            edge[it, n] = part[it, pl.ds(span + a, HALO)] + (part_in[it, 0, rows_at] + part_in[it, 1, rows_at])
            edges.append(Copy(side, edge.at[it, n], edge_in.at[it, 1 - n]))
        for c in shares[2]:
            c.arrive()
        mid = pl.ds(HALO, depth)
        correction = part[it, own] + (part_in[it, 0, mid] + part_in[it, 1, mid])
        for c in edges:
            c.arrive()
        rest = jnp.zeros((depth - HALO, width), F32)
        correction = correction + jnp.concatenate([edge_in[it, 0], rest], axis=0)
        correction = correction + jnp.concatenate([rest, edge_in[it, 1]], axis=0)
        new = cur[it, own] * correction * (1.0 / views)
        if it + 1 < ITERS:
            cur[it + 1, own] = new
        else:
            out[...] = new
        for c in shares[0] + shares[1] + shares[2] + edges:
            c.leave()


def shards(groups, lanes, estimate, view_lines, line_owner, line_target, view_shift, psf_x, psf_yz):
    _, depth, width = estimate.shape
    views, n, _ = view_lines.shape
    cap = 2 * n // groups
    slots, span, all_rows = views * cap, depth + 2 * HALO, views * depth
    codes = (line_owner[:, :, 0] * depth + line_target).reshape(1, views * n)
    vmem, smem = pl.BlockSpec(memory_space=pltpu.VMEM), pl.BlockSpec(memory_space=pltpu.SMEM)
    columns = -(-3 * span // 128) * 128
    copies = 18 * ITERS
    out = pl.pallas_call(
        functools.partial(kernel, groups, lanes, views, cap),
        out_shape=jax.ShapeDtypeStruct((depth, width), F32),
        in_specs=[vmem, vmem, vmem, smem, smem, smem],
        out_specs=vmem,
        scratch_shapes=[
            pltpu.VMEM((groups, slots, width), F32),
            pltpu.VMEM((groups, slots, width), F32),
            pltpu.VMEM((groups, 1, groups * slots), F32),
            pltpu.VMEM((groups, 1, groups * slots), F32),
            pltpu.VMEM((ITERS, columns, width), F32),
            pltpu.VMEM((ITERS, columns, width), F32),
            pltpu.VMEM((ITERS, 2, span, width), F32),
            pltpu.VMEM((ITERS, 2, HALO, width), F32),
            pltpu.VMEM((ITERS, 2, HALO, width), F32),
            pltpu.VMEM((2 * all_rows, columns), BF16),
            pltpu.VMEM((columns, 2 * all_rows), BF16),
            pltpu.VMEM((columns, all_rows), BF16),
            pltpu.VMEM((views, 256, 256), BF16),
            pltpu.VMEM((views, 256, 256), BF16),
            pltpu.VMEM((all_rows, width), F32),
            pltpu.VMEM((all_rows, width), F32),
            pltpu.VMEM((all_rows, width), F32),
            pltpu.SemaphoreType.DMA((copies,)),
            pltpu.SemaphoreType.DMA((copies,)),
            pltpu.SemaphoreType.DMA((groups,)),
            pltpu.SemaphoreType.DMA((groups,)),
            pltpu.SemaphoreType.DMA((groups,)),
            pltpu.SemaphoreType.DMA((groups,)),
        ],
        compiler_params=pltpu.CompilerParams(
            collective_id=0, has_side_effects=True, vmem_limit_bytes=40 << 20
        ),
    )(
        estimate.reshape(depth, width),
        view_lines.reshape(views * n, width),
        codes,
        view_shift,
        psf_x,
        psf_yz,
    )
    return out.reshape(estimate.shape)


def solution(mesh):
    placed = (
        P("grp", "lane", None),
        P(None, ("grp", "lane"), None),
        P(None, ("grp", "lane"), None),
        P(None, ("grp", "lane")),
        P(),
        P(),
        P(),
    )
    return jax.shard_map(
        functools.partial(shards, mesh.shape["grp"], mesh.shape["lane"]),
        mesh=mesh, in_specs=placed, out_specs=P("grp", "lane", None), check_vma=False,
    )
```

```python
import functools

import jax
import jax.numpy as jnp
from jax import lax
from jax.experimental import pallas as pl
from jax.experimental.pallas import tpu as pltpu
from jax.sharding import PartitionSpec as P

ITERS = 2
HALO = 24
MESH = pl.DeviceIdType.MESH
F32, BF16 = jnp.float32, jnp.bfloat16


def halves(x):
    high = x.astype(BF16)
    return high, (x - high.astype(F32)).astype(BF16)


def dot(a, b):
    return jnp.dot(a, b, preferred_element_type=F32)


def iota(shape, dim):
    return lax.broadcasted_iota(jnp.int32, shape, dim)


def total_of(ref, *at, size):
    summed = ref[(*at, 0)]
    for k in range(1, size):
        summed = summed + ref[(*at, k)]
    return summed


def along_y(x, taps):
    rows, width = x.shape
    blocks = width // 128
    padded = pltpu.roll(jnp.concatenate([x, jnp.zeros((rows, 128), F32)], axis=1), 64, 1)
    high, low = halves(padded)
    windows = [part[:, 128 * b : 128 * b + 256] for part in (high, low) for b in range(blocks)]
    r = dot(jnp.concatenate(windows, axis=0), taps)
    n = blocks * rows
    summed = r[:n, :128] + (r[:n, 128:] + r[n:, :128])
    return jnp.concatenate([summed[rows * b : rows * (b + 1)] for b in range(blocks)], axis=1)


def kernel(groups, lanes, views, cap, est_at, lines_at, owner_at, target_at, shift_at, psf_x_at, psf_yz_at, out,
           lines, owners, targets, shift, psf_x, psf_yz, load_sem,
           outgoing, arrived, meta_out, meta_in, cur, part, part_in, edge, edge_in, beyond, passing,
           m_fwd, m_adj, m_adj_low, t_fwd, t_adj, observed, blurred, spread,
           send_sem, recv_sem, a2a_send, a2a_recv, meta_send, meta_recv):
    p, l = lax.axis_index("grp"), lax.axis_index("lane")
    depth, width = est_at.shape
    taps = psf_yz.shape[2]
    reach = (taps - 1) // 2
    slots = views * cap
    span = depth + 2 * HALO
    all_rows = views * depth
    chunk = min(256, width)
    has = {"before": p > 0, "after": p < groups - 1, "up": l > 0, "down": l < lanes - 1}
    where = {
        "before": (jnp.maximum(p - 1, 0), l),
        "after": (jnp.minimum(p + 1, groups - 1), l),
        "up": (p, jnp.maximum(l - 1, 0)),
        "down": (p, jnp.minimum(l + 1, lanes - 1)),
    }
    opposite = {"before": "after", "after": "before", "up": "down", "down": "up"}
    counter = [0]

    class Copy:
        def __init__(self, to, since, target, src, dst):
            at = counter[0]
            counter[0] += 1
            self.to, self.since = to, since
            self.copy = pltpu.make_async_remote_copy(
                src_ref=src, dst_ref=dst, send_sem=send_sem.at[at], recv_sem=recv_sem.at[at],
                device_id=target, device_id_type=MESH,
            )
            pl.when(self.to)(self.copy.start)

        def arrive(self):
            pl.when(self.since)(self.copy.wait_recv)

        def leave(self):
            pl.when(self.to)(self.copy.wait_send)

    def beside(side, src, dst):
        return Copy(has[side], has[opposite[side]], where[side], src, dst)

    high_lane = lanes // 2
    low_lane = high_lane - 1
    far_low, far_high = high_lane - 4, high_lane + 3
    near = {"up": has["up"] & (l != high_lane), "down": has["down"] & (l != low_lane)}

    def between(a, b, src, dst):
        return Copy(l == a, l == b, (p, jnp.int32(b)), src, dst)

    barrier = pltpu.get_barrier_semaphore()
    for k in range(1, groups):
        pl.semaphore_signal(barrier, inc=1, device_id=(lax.rem(p + k, groups), l), device_id_type=MESH)
    expected = groups - 1
    greeted = [(has[side], where[side]) for side in ("up", "down")]
    for a, b in ((far_low, low_lane), (far_low, high_lane), (low_lane - 1, high_lane),
                 (far_high, high_lane), (far_high, low_lane), (high_lane + 1, low_lane)):
        greeted += [(l == a, (p, jnp.int32(b))), (l == b, (p, jnp.int32(a)))]
    for cond, device in greeted:
        expected = expected + jnp.where(cond, 1, 0)

        @pl.when(cond)
        def _(device=device):
            pl.semaphore_signal(barrier, inc=1, device_id=device, device_id_type=MESH)

    own = pl.ds(span + HALO, depth)
    loads = [
        pltpu.make_async_copy(src, dst, load_sem.at[n])
        for n, (src, dst) in enumerate((
            (owner_at, owners), (target_at, targets), (lines_at, lines), (est_at, cur.at[0, own]),
            (shift_at, shift), (psf_x_at, psf_x), (psf_yz_at, psf_yz),
        ))
    ]
    for c in loads:
        c.start()

    for it in range(ITERS):
        cur[it, 3 * span :] = jnp.zeros((cur.shape[1] - 3 * span, width), F32)

    @pl.when(p == 0)
    def _():
        for it in range(ITERS):
            cur[it, 0:span] = jnp.zeros((span, width), F32)
            part_in[it, 0] = jnp.zeros((span, width), F32)

    @pl.when(p == groups - 1)
    def _():
        for it in range(ITERS):
            cur[it, 2 * span : 3 * span] = jnp.zeros((span, width), F32)
            part_in[it, 1] = jnp.zeros((span, width), F32)

    @pl.when(l == 0)
    def _():
        for it in range(ITERS):
            cur[it, span : span + HALO] = jnp.zeros((HALO, width), F32)
            edge_in[it, 0] = jnp.zeros((HALO, width), F32)

    @pl.when(l == lanes - 1)
    def _():
        for it in range(ITERS):
            cur[it, 2 * span - HALO : 2 * span] = jnp.zeros((HALO, width), F32)
            edge_in[it, 1] = jnp.zeros((HALO, width), F32)

    for c in loads:
        c.wait()

    n_lines = lines.shape[0]
    per_view = n_lines // views
    owner = jnp.concatenate([owners[v : v + 1, :] for v in range(views)], axis=1)
    landing = jnp.concatenate([targets[v : v + 1, :] for v in range(views)], axis=1)
    line_at = iota((1, n_lines), 1)
    view = line_at // per_view
    key = view * groups + owner
    wide = jnp.broadcast_to(key, (n_lines, n_lines))
    earlier = iota((n_lines, n_lines), 0) < iota((n_lines, n_lines), 1)
    same = jnp.where((wide == wide.T) & earlier, 1.0, 0.0)
    rank = jnp.sum(same, axis=0, keepdims=True).astype(jnp.int32)
    in_block = view * cap + rank
    picks = jnp.where(iota((groups * slots, n_lines), 0) == owner * slots + in_block, 1.0, 0.0).astype(BF16)
    named = jnp.where(iota((groups, n_lines), 0) == owner, view * depth + landing + 1, 0)
    place = jnp.where(iota((groups * slots, n_lines), 0) == p * slots + in_block, 1.0, 0.0).astype(BF16)
    meta = lax.dot_general(
        named.astype(F32).astype(BF16), place, (((1,), (1,)), ((), ())), preferred_element_type=F32
    )
    for g in range(groups):
        meta_out[g] = meta[g : g + 1]
    picks2 = jnp.concatenate([picks, picks], axis=1)
    for at in range(0, width, chunk):
        high, low = halves(lines[:, at : at + chunk])
        packed = dot(picks2, jnp.concatenate([high, low], axis=0))
        outgoing[:, :, at : at + chunk] = packed.reshape(groups, slots, chunk)

    pl.semaphore_wait(barrier, expected)

    departed = []

    def widen_start(it):
        now = cur.at[it]
        lo, hi = span, 2 * span
        sides = near if it > 0 else has
        ups = [
            Copy(sides["up"], sides["down"], where["up"], now.at[lo + HALO : lo + 2 * HALO], now.at[hi - HALO : hi]),
            Copy(sides["down"], sides["up"], where["down"], now.at[hi - 2 * HALO : hi - HALO], now.at[lo : lo + HALO]),
        ]
        own_rows = now.at[lo + HALO : hi - HALO]
        mids = [
            beside("before", own_rows, now.at[2 * span + HALO : 3 * span - HALO]),
            beside("after", own_rows, now.at[HALO : span - HALO]),
        ]
        return ups, mids

    def widen_finish(it, ups, mids):
        now = cur.at[it]
        for c, at in ((ups[1], 0), (ups[0], span - HALO)):
            c.arrive()
            got = now.at[span + at : span + at + HALO]
            mids.append(beside("before", got, now.at[2 * span + at : 2 * span + at + HALO]))
            mids.append(beside("after", got, now.at[at : at + HALO]))
        for c in mids:
            c.arrive()
        departed.extend(ups + mids)

    ups, mids = widen_start(0)
    routes = []
    for k in sorted(range(1, groups), key=lambda k: -min(k, groups - k)):
        to = (lax.rem(p + k, groups), l)
        for src, dst, sent, got in (
            (meta_out.at[to[0]], meta_in.at[p], meta_send, meta_recv),
            (outgoing.at[to[0]], arrived.at[p], a2a_send, a2a_recv),
        ):
            c = pltpu.make_async_remote_copy(
                src_ref=src, dst_ref=dst, send_sem=sent.at[k], recv_sem=got.at[k],
                device_id=to, device_id_type=MESH,
            )
            c.start()
            routes.append(c)
    arrived[p] = outgoing[p]
    meta_in[p] = meta_out[p]

    columns = m_fwd.shape[1]
    column = iota((depth, columns), 1)
    plane = jnp.where(column < span, 0, jnp.where(column < 2 * span, 1, 2))
    tap_at = iota((depth, columns), 0) + (reach + HALO) - (column - plane * span)
    tap_at = jnp.where(column < 3 * span, tap_at, -1)
    blocks = []
    for v in range(views):
        acc = jnp.zeros((depth, columns), F32)
        for t in range(taps):
            acc = jnp.where(tap_at == t, psf_yz[v, 1, t], acc)
        across = jnp.where(plane == 0, psf_x[v, 2], jnp.where(plane == 1, psf_x[v, 1], psf_x[v, 0]))
        norm = jnp.full((1, columns), total_of(psf_yz, v, 1, size=taps)) * jnp.full(
            (1, columns), total_of(psf_x, v, size=3)
        )
        blocks.append(acc * across / norm)
    matrix = jnp.concatenate(blocks, axis=0)
    high, low = halves(matrix)
    m_fwd[0:all_rows] = high
    m_fwd[all_rows:] = low
    high, low = halves(matrix.T)
    m_adj[:, 0:all_rows] = high
    m_adj[:, all_rows:] = high
    m_adj_low[...] = low

    rows = 32

    def band(step, carry):
        i = iota((rows, 128), 0) + step * rows
        j = iota((rows, 128), 1)
        for v in range(views):
            norm = jnp.full((1, 128), total_of(psf_yz, v, 0, size=taps))
            for ref, at in ((t_fwd, j - i + (64 + reach + shift[v])), (t_adj, i - j + (reach - 64 + shift[v]))):
                acc = jnp.zeros((rows, 128), F32)
                for t in range(taps):
                    acc = jnp.where(at == t, psf_yz[v, 0, t], acc)
                high, low = halves(acc / norm)
                ref[v, pl.ds(pl.multiple_of(step * rows, rows), rows), 0:128] = high
                ref[v, pl.ds(pl.multiple_of(step * rows, rows), rows), 128:256] = low
        return carry

    lax.fori_loop(0, 256 // rows, band, 0)

    def blur(it):
        for at in range(0, width, chunk):
            high, low = halves(cur[it, :, at : at + chunk])
            r = dot(m_fwd[...], high)
            spread[:, at : at + chunk] = r[:all_rows] + (r[all_rows:] + dot(m_fwd[0:all_rows], low))
        for v in range(views):
            blurred[v * depth : (v + 1) * depth] = along_y(spread[v * depth : (v + 1) * depth], t_fwd[v])

    widen_finish(0, ups, mids)
    blur(0)

    for c in routes:
        c.wait()
    marks = jnp.sum(meta_in[...], axis=0)
    lands = jnp.where(iota((all_rows, groups * slots), 0) + 1 == marks.astype(jnp.int32), 1.0, 0.0).astype(BF16)
    for at in range(0, width, chunk):
        high, low = halves(arrived[:, :, at : at + chunk].reshape(groups * slots, chunk))
        observed[:, at : at + chunk] = dot(lands, high) + dot(lands, low)

    for it in range(ITERS):
        if it > 0:
            widen_finish(it, *widen_start(it))
            blur(it)
        y = iota((depth, width), 1)
        for v in range(views):
            at = pl.ds(v * depth, depth)
            seen = y + shift[v]
            quotient = jnp.where((seen >= 0) & (seen < width), observed[at] / blurred[at], 0.0)
            spread[at] = along_y(quotient, t_adj[v])
        for at in range(0, width, chunk):
            high, low = halves(spread[:, at : at + chunk])
            r = dot(m_adj[...], jnp.concatenate([high, low], axis=0)) + dot(m_adj_low[...], high)
            part[it, :, at : at + chunk] = r
        mine, theirs = part.at[it], part_in.at[it]
        shares = []
        for rows_at in ((0, HALO), (span - HALO, span), (HALO, span - HALO)):
            a, b = rows_at
            shares.append([
                beside("before", mine.at[a:b], theirs.at[1, a:b]),
                beside("after", mine.at[2 * span + a : 2 * span + b], theirs.at[0, a:b]),
            ])
        edges, across = [], []
        for n, (side, a) in enumerate((("up", 0), ("down", span - HALO))):
            for c in shares[n]:
                c.arrive()
            rows_at = pl.ds(a, HALO)
            edge[it, n] = part[it, pl.ds(span + a, HALO)] + (part_in[it, 0, rows_at] + part_in[it, 1, rows_at])
            edges.append(beside(side, edge.at[it, n], edge_in.at[it, 1 - n]))
        if it + 1 < ITERS:
            across += [
                between(low_lane - 1, high_lane, edge.at[it, 1], beyond.at[0]),
                between(high_lane + 1, low_lane, edge.at[it, 0], beyond.at[0]),
            ]
        for c in shares[2]:
            c.arrive()
        mid = pl.ds(HALO, depth)
        correction = part[it, own] + (part_in[it, 0, mid] + part_in[it, 1, mid])
        if it + 1 < ITERS:
            passing[0] = correction
            first = [
                between(low_lane, far_low, passing.at[0, depth - HALO :], passing.at[1, 0:HALO]),
                between(high_lane, far_high, passing.at[0, 0:HALO], passing.at[1, 0:HALO]),
            ]
            for c, a, b in ((first[0], far_low, high_lane), (first[1], far_high, low_lane)):
                c.arrive()
                across.append(between(a, b, passing.at[1, 0:HALO], beyond.at[1]))
        for c in edges:
            c.arrive()
        rest = jnp.zeros((depth - HALO, width), F32)
        correction = correction + jnp.concatenate([edge_in[it, 0], rest], axis=0)
        correction = correction + jnp.concatenate([rest, edge_in[it, 1]], axis=0)
        new = cur[it, own] * correction * (1.0 / views)
        if it + 1 < ITERS:
            cur[it + 1, own] = new
            for c in across:
                c.arrive()
            overlap = 2 * HALO - depth
            blank = jnp.zeros((depth - HALO, width), F32)
            for me, n, a in ((high_lane, 0, 0), (low_lane, 1, span - HALO)):

                @pl.when(l == me)
                def _(n=n, a=a, it=it):
                    got = beyond[0]
                    kept = (
                        jnp.concatenate([got[HALO - overlap :], blank], axis=0)
                        if n == 0
                        else jnp.concatenate([blank, got[:overlap]], axis=0)
                    )
                    total = edge[it, n] + (beyond[1] + kept)
                    rows_at = pl.ds(span + a, HALO)
                    cur[it + 1, rows_at] = cur[it, rows_at] * total * (1.0 / views)

            departed.extend(first + across)
        else:
            out[...] = new
        departed.extend(shares[0] + shares[1] + shares[2] + edges)
    for c in departed:
        c.leave()


def shards(groups, lanes, estimate, view_lines, line_owner, line_target, view_shift, psf_x, psf_yz):
    _, depth, width = estimate.shape
    views, n, _ = view_lines.shape
    cap = 2 * n // groups
    slots, span, all_rows = views * cap, depth + 2 * HALO, views * depth
    hbm = pl.BlockSpec(memory_space=pltpu.HBM)
    columns = -(-3 * span // 128) * 128
    copies = 18 * ITERS + 6
    vmem = lambda *shape: pltpu.VMEM(shape, F32)
    dma = lambda n: pltpu.SemaphoreType.DMA((n,))
    out = pl.pallas_call(
        functools.partial(kernel, groups, lanes, views, cap),
        out_shape=jax.ShapeDtypeStruct((depth, width), F32),
        in_specs=[hbm] * 7,
        out_specs=pl.BlockSpec(memory_space=pltpu.VMEM),
        scratch_shapes=[
            vmem(views * n, width),
            pltpu.VMEM((views, n), jnp.int32),
            pltpu.VMEM((views, n), jnp.int32),
            pltpu.SMEM(view_shift.shape, jnp.int32),
            pltpu.SMEM(psf_x.shape, F32),
            pltpu.SMEM(psf_yz.shape, F32),
            dma(7),
            vmem(groups, slots, width),
            vmem(groups, slots, width),
            vmem(groups, 1, groups * slots),
            vmem(groups, 1, groups * slots),
            vmem(ITERS, columns, width),
            vmem(ITERS, columns, width),
            vmem(ITERS, 2, span, width),
            vmem(ITERS, 2, HALO, width),
            vmem(ITERS, 2, HALO, width),
            vmem(2, HALO, width),
            vmem(2, depth, width),
            pltpu.VMEM((2 * all_rows, columns), BF16),
            pltpu.VMEM((columns, 2 * all_rows), BF16),
            pltpu.VMEM((columns, all_rows), BF16),
            pltpu.VMEM((views, 256, 256), BF16),
            pltpu.VMEM((views, 256, 256), BF16),
            vmem(all_rows, width),
            vmem(all_rows, width),
            vmem(all_rows, width),
            dma(copies),
            dma(copies),
            dma(groups),
            dma(groups),
            dma(groups),
            dma(groups),
        ],
        compiler_params=pltpu.CompilerParams(
            collective_id=0, has_side_effects=True, vmem_limit_bytes=64 << 20
        ),
    )(
        estimate.reshape(depth, width),
        view_lines.reshape(views * n, width),
        line_owner[:, :, 0],
        line_target,
        view_shift,
        psf_x,
        psf_yz,
    )
    return out.reshape(estimate.shape)


def solution(mesh):
    placed = (
        P("grp", "lane", None),
        P(None, ("grp", "lane"), None),
        P(None, ("grp", "lane"), None),
        P(None, ("grp", "lane")),
        P(),
        P(),
        P(),
    )
    return jax.shard_map(
        functools.partial(shards, mesh.shape["grp"], mesh.shape["lane"]),
        mesh=mesh, in_specs=placed, out_specs=P("grp", "lane", None), check_vma=False,
    )
```

```python
import functools

import jax
import jax.numpy as jnp
from jax import lax
from jax.experimental import pallas as pl
from jax.experimental.pallas import tpu as pltpu
from jax.sharding import PartitionSpec as P

ITERS = 2
AHEAD = 1
HALO = 24
MESH = pl.DeviceIdType.MESH
F32, BF16 = jnp.float32, jnp.bfloat16


def halves(x):
    high = x.astype(BF16)
    return high, (x - high.astype(F32)).astype(BF16)


def dot(a, b):
    return jnp.dot(a, b, preferred_element_type=F32)


def iota(shape, dim):
    return lax.broadcasted_iota(jnp.int32, shape, dim)


def total_of(ref, *at, size):
    summed = ref[(*at, 0)]
    for k in range(1, size):
        summed = summed + ref[(*at, k)]
    return summed


def along_y(x, taps):
    rows, width = x.shape
    blocks = width // 128
    padded = pltpu.roll(jnp.concatenate([x, jnp.zeros((rows, 128), F32)], axis=1), 64, 1)
    high, low = halves(padded)
    windows = [part[:, 128 * b : 128 * b + 256] for part in (high, low) for b in range(blocks)]
    r = dot(jnp.concatenate(windows, axis=0), taps)
    n = blocks * rows
    summed = r[:n, :128] + (r[:n, 128:] + r[n:, :128])
    return jnp.concatenate([summed[rows * b : rows * (b + 1)] for b in range(blocks)], axis=1)


def relays(groups, lanes):
    middle = groups // 2
    if lanes < 32 or groups < 8:
        return [(0, middle)], lanes // 2 - 1
    plan = [(0, middle+0), (0, middle-1), (0, middle+1), (0, middle+2), (1, middle+0)]
    return plan, lanes // 2 - 6


def kernel(groups, lanes, views, cap, est_at, lines_at, owner_at, target_at, shift_at, psf_x_at, psf_yz_at, out,
           lines, owners, targets, shift, psf_x, psf_yz, load_sem,
           outgoing, arrived, meta_out, meta_in, cur, part, part_in, edge, edge_in, beyond, passing, relayed,
           m_fwd, m_adj, m_adj_low, t_fwd, t_adj, observed, blurred, spread,
           send_sem, recv_sem, relay_send, a2a_send, a2a_recv, meta_send, meta_recv):
    p, l = lax.axis_index("grp"), lax.axis_index("lane")
    depth, width = est_at.shape
    taps = psf_yz.shape[2]
    reach = (taps - 1) // 2
    slots = views * cap
    span = depth + 2 * HALO
    all_rows = views * depth
    chunk = min(256, width)
    has = {"before": p > 0, "after": p < groups - 1, "up": l > 0, "down": l < lanes - 1}
    where = {
        "before": (jnp.maximum(p - 1, 0), l),
        "after": (jnp.minimum(p + 1, groups - 1), l),
        "up": (p, jnp.maximum(l - 1, 0)),
        "down": (p, jnp.minimum(l + 1, lanes - 1)),
    }
    opposite = {"before": "after", "after": "before", "up": "down", "down": "up"}
    counter = [0]

    class Copy:
        def __init__(self, to, since, target, src, dst):
            at = counter[0]
            counter[0] += 1
            self.to, self.since = to, since
            self.copy = pltpu.make_async_remote_copy(
                src_ref=src, dst_ref=dst, send_sem=send_sem.at[at], recv_sem=recv_sem.at[at],
                device_id=target, device_id_type=MESH,
            )
            pl.when(self.to)(self.copy.start)

        def arrive(self):
            pl.when(self.since)(self.copy.wait_recv)

        def leave(self):
            pl.when(self.to)(self.copy.wait_send)

    def beside(side, src, dst):
        return Copy(has[side], has[opposite[side]], where[side], src, dst)

    high_lane = lanes // 2
    low_lane = high_lane - 1
    far_low, far_high = high_lane - 4, high_lane + 3
    near = {"up": has["up"] & (l != high_lane), "down": has["down"] & (l != low_lane)}

    def between(a, b, src, dst):
        return Copy(l == a, l == b, (p, jnp.int32(b)), src, dst)

    half = lanes // 2
    from_end = jnp.minimum(l, lanes - 1 - l)
    plan, pool = relays(groups, lanes)

    def in_half(lane):
        return jnp.where(l < half, lane, lanes - 1 - lane)

    def relay_of(plane, n):
        return lax.rem(len(plan) * plane + n, pool)

    barrier = pltpu.get_barrier_semaphore()
    for k in range(1, groups):
        pl.semaphore_signal(barrier, inc=1, device_id=(lax.rem(p + k, groups), l), device_id_type=MESH)
    expected = groups - 1
    greeted = [(has[side], where[side]) for side in ("up", "down")]
    for a, b in ((far_low, low_lane), (far_low, high_lane), (low_lane - 1, high_lane),
                 (far_high, high_lane), (far_high, low_lane), (high_lane + 1, low_lane)):
        greeted += [(l == a, (p, jnp.int32(b))), (l == b, (p, jnp.int32(a)))]
    for cond, _ in greeted:
        expected = expected + jnp.where(cond, 1, 0)
    for n, (distance, k) in enumerate(plan):
        source = half - 1 - distance
        is_source, is_relay = from_end == source, from_end == relay_of(p, n)
        expected = expected + jnp.where(is_source, 1, 0) + jnp.where(is_relay, 1, 0)
        sender = lax.rem(p + groups - k, groups)
        greeted.append((is_relay, (p, in_half(source))))
        greeted.append((is_source, (sender, in_half(relay_of(sender, n)))))
    for cond, device in greeted:

        @pl.when(cond)
        def _(device=device):
            pl.semaphore_signal(barrier, inc=1, device_id=device, device_id_type=MESH)

    own = pl.ds(span + HALO, depth)
    loads = [
        pltpu.make_async_copy(src, dst, load_sem.at[n])
        for n, (src, dst) in enumerate((
            (owner_at, owners), (target_at, targets), (lines_at, lines), (est_at, cur.at[0, own]),
            (shift_at, shift), (psf_x_at, psf_x), (psf_yz_at, psf_yz),
        ))
    ]
    for c in loads:
        c.start()

    for it in range(ITERS):
        cur[it, 3 * span :] = jnp.zeros((cur.shape[1] - 3 * span, width), F32)

    @pl.when(p == 0)
    def _():
        for it in range(ITERS):
            cur[it, 0:span] = jnp.zeros((span, width), F32)
            part_in[it, 0] = jnp.zeros((span, width), F32)

    @pl.when(p == groups - 1)
    def _():
        for it in range(ITERS):
            cur[it, 2 * span : 3 * span] = jnp.zeros((span, width), F32)
            part_in[it, 1] = jnp.zeros((span, width), F32)

    @pl.when(l == 0)
    def _():
        for it in range(ITERS):
            cur[it, span : span + HALO] = jnp.zeros((HALO, width), F32)
            edge_in[it, 0] = jnp.zeros((HALO, width), F32)

    @pl.when(l == lanes - 1)
    def _():
        for it in range(ITERS):
            cur[it, 2 * span - HALO : 2 * span] = jnp.zeros((HALO, width), F32)
            edge_in[it, 1] = jnp.zeros((HALO, width), F32)

    for c in loads:
        c.wait()

    n_lines = lines.shape[0]
    per_view = n_lines // views
    owner = jnp.concatenate([owners[v : v + 1, :] for v in range(views)], axis=1)
    landing = jnp.concatenate([targets[v : v + 1, :] for v in range(views)], axis=1)
    line_at = iota((1, n_lines), 1)
    view = line_at // per_view
    key = view * groups + owner
    wide = jnp.broadcast_to(key, (n_lines, n_lines))
    earlier = iota((n_lines, n_lines), 0) < iota((n_lines, n_lines), 1)
    same = jnp.where((wide == wide.T) & earlier, 1.0, 0.0)
    rank = jnp.sum(same, axis=0, keepdims=True).astype(jnp.int32)
    in_block = view * cap + rank
    picks = jnp.where(iota((groups * slots, n_lines), 0) == owner * slots + in_block, 1.0, 0.0).astype(BF16)
    named = jnp.where(iota((groups, n_lines), 0) == owner, view * depth + landing + 1, 0)
    place = jnp.where(iota((groups * slots, n_lines), 0) == p * slots + in_block, 1.0, 0.0).astype(BF16)
    meta = lax.dot_general(
        named.astype(F32).astype(BF16), place, (((1,), (1,)), ((), ())), preferred_element_type=F32
    )
    for g in range(groups):
        meta_out[g] = meta[g : g + 1]
    picks2 = jnp.concatenate([picks, picks], axis=1)
    for at in range(0, width, chunk):
        high, low = halves(lines[:, at : at + chunk])
        packed = dot(picks2, jnp.concatenate([high, low], axis=0))
        outgoing[:, :, at : at + chunk] = packed.reshape(groups, slots, chunk)

    pl.semaphore_wait(barrier, expected)

    def widen_start(it):
        now = cur.at[it]
        lo, hi = span, 2 * span
        sides = near if it > 0 else has
        ups = [
            Copy(sides["up"], sides["down"], where["up"], now.at[lo + HALO : lo + 2 * HALO], now.at[hi - HALO : hi]),
            Copy(sides["down"], sides["up"], where["down"], now.at[hi - 2 * HALO : hi - HALO], now.at[lo : lo + HALO]),
        ]
        own_rows = now.at[lo + HALO : hi - HALO]
        mids = [
            beside("before", own_rows, now.at[2 * span + HALO : 3 * span - HALO]),
            beside("after", own_rows, now.at[HALO : span - HALO]),
        ]
        return ups, mids

    def widen_finish(it, ups, mids):
        now = cur.at[it]
        for c, at in ((ups[1], 0), (ups[0], span - HALO)):
            c.arrive()
            got = now.at[span + at : span + at + HALO]
            mids.append(beside("before", got, now.at[2 * span + at : 2 * span + at + HALO]))
            mids.append(beside("after", got, now.at[at : at + HALO]))
        for c in mids:
            c.arrive()
        departed.extend(ups + mids)

    departed = []
    first_legs = [
        Copy(
            from_end == half - 1 - distance, from_end == relay_of(p, n), (p, in_half(relay_of(p, n))),
            outgoing.at[lax.rem(p + k, groups)], relayed.at[n],
        )
        for n, (distance, k) in enumerate(plan)
    ]
    ups, mids = widen_start(0)
    routes = []

    def pass_on():
        for n, (distance, k) in enumerate(plan):
            first_legs[n].arrive()
            second = pltpu.make_async_remote_copy(
                src_ref=relayed.at[n], dst_ref=arrived.at[p], send_sem=relay_send.at[n], recv_sem=a2a_recv.at[k],
                device_id=(lax.rem(p + k, groups), in_half(half - 1 - distance)), device_id_type=MESH,
            )
            is_relay = from_end == relay_of(p, n)
            pl.when(is_relay)(second.start)
            routes.append((None, is_relay, second))

    order = sorted(range(1, groups), key=lambda k: -min(k, groups - k))
    for turn, k in enumerate(order):
        if turn == AHEAD % len(order):
            pass_on()
        to = (lax.rem(p + k, groups), l)
        direct = p >= 0
        for distance, offset in plan:
            if offset == k:
                direct = direct & (from_end != half - 1 - distance)
        for always, src, dst, sent, got in (
            (True, meta_out.at[to[0]], meta_in.at[p], meta_send, meta_recv),
            (False, outgoing.at[to[0]], arrived.at[p], a2a_send, a2a_recv),
        ):
            c = pltpu.make_async_remote_copy(
                src_ref=src, dst_ref=dst, send_sem=sent.at[k], recv_sem=got.at[k],
                device_id=to, device_id_type=MESH,
            )
            if always:
                c.start()
            else:
                pl.when(direct)(c.start)
            routes.append((always, direct, c))
    arrived[p] = outgoing[p]
    meta_in[p] = meta_out[p]

    columns = m_fwd.shape[1]
    column = iota((depth, columns), 1)
    plane = jnp.where(column < span, 0, jnp.where(column < 2 * span, 1, 2))
    tap_at = iota((depth, columns), 0) + (reach + HALO) - (column - plane * span)
    tap_at = jnp.where(column < 3 * span, tap_at, -1)
    blocks = []
    for v in range(views):
        acc = jnp.zeros((depth, columns), F32)
        for t in range(taps):
            acc = jnp.where(tap_at == t, psf_yz[v, 1, t], acc)
        across = jnp.where(plane == 0, psf_x[v, 2], jnp.where(plane == 1, psf_x[v, 1], psf_x[v, 0]))
        norm = jnp.full((1, columns), total_of(psf_yz, v, 1, size=taps)) * jnp.full(
            (1, columns), total_of(psf_x, v, size=3)
        )
        blocks.append(acc * across / norm)
    matrix = jnp.concatenate(blocks, axis=0)
    high, low = halves(matrix)
    m_fwd[0:all_rows] = high
    m_fwd[all_rows:] = low
    high, low = halves(matrix.T)
    m_adj[:, 0:all_rows] = high
    m_adj[:, all_rows:] = high
    m_adj_low[...] = low

    rows = 32

    def band(step, carry):
        i = iota((rows, 128), 0) + step * rows
        j = iota((rows, 128), 1)
        for v in range(views):
            norm = jnp.full((1, 128), total_of(psf_yz, v, 0, size=taps))
            for ref, at in ((t_fwd, j - i + (64 + reach + shift[v])), (t_adj, i - j + (reach - 64 + shift[v]))):
                acc = jnp.zeros((rows, 128), F32)
                for t in range(taps):
                    acc = jnp.where(at == t, psf_yz[v, 0, t], acc)
                high, low = halves(acc / norm)
                ref[v, pl.ds(pl.multiple_of(step * rows, rows), rows), 0:128] = high
                ref[v, pl.ds(pl.multiple_of(step * rows, rows), rows), 128:256] = low
        return carry

    lax.fori_loop(0, 256 // rows, band, 0)

    def blur(it):
        for at in range(0, width, chunk):
            high, low = halves(cur[it, :, at : at + chunk])
            r = dot(m_fwd[...], high)
            spread[:, at : at + chunk] = r[:all_rows] + (r[all_rows:] + dot(m_fwd[0:all_rows], low))
        for v in range(views):
            blurred[v * depth : (v + 1) * depth] = along_y(spread[v * depth : (v + 1) * depth], t_fwd[v])

    widen_finish(0, ups, mids)
    blur(0)

    for always, sent, c in routes:
        if always is not None:
            c.wait_recv()
    marks = jnp.sum(meta_in[...], axis=0)
    lands = jnp.where(iota((all_rows, groups * slots), 0) + 1 == marks.astype(jnp.int32), 1.0, 0.0).astype(BF16)
    for at in range(0, width, chunk):
        high, low = halves(arrived[:, :, at : at + chunk].reshape(groups * slots, chunk))
        observed[:, at : at + chunk] = dot(lands, high) + dot(lands, low)

    for it in range(ITERS):
        if it > 0:
            widen_finish(it, *widen_start(it))
            blur(it)
        y = iota((depth, width), 1)
        for v in range(views):
            at = pl.ds(v * depth, depth)
            seen = y + shift[v]
            quotient = jnp.where((seen >= 0) & (seen < width), observed[at] / blurred[at], 0.0)
            spread[at] = along_y(quotient, t_adj[v])
        for at in range(0, width, chunk):
            high, low = halves(spread[:, at : at + chunk])
            r = dot(m_adj[...], jnp.concatenate([high, low], axis=0)) + dot(m_adj_low[...], high)
            part[it, :, at : at + chunk] = r
        mine, theirs = part.at[it], part_in.at[it]
        shares = []
        for rows_at in ((0, HALO), (span - HALO, span), (HALO, span - HALO)):
            a, b = rows_at
            shares.append([
                beside("before", mine.at[a:b], theirs.at[1, a:b]),
                beside("after", mine.at[2 * span + a : 2 * span + b], theirs.at[0, a:b]),
            ])
        edges, across = [], []
        for n, (side, a) in enumerate((("up", 0), ("down", span - HALO))):
            for c in shares[n]:
                c.arrive()
            rows_at = pl.ds(a, HALO)
            edge[it, n] = part[it, pl.ds(span + a, HALO)] + (part_in[it, 0, rows_at] + part_in[it, 1, rows_at])
            edges.append(beside(side, edge.at[it, n], edge_in.at[it, 1 - n]))
        if it + 1 < ITERS:
            across += [
                between(low_lane - 1, high_lane, edge.at[it, 1], beyond.at[0]),
                between(high_lane + 1, low_lane, edge.at[it, 0], beyond.at[0]),
            ]
        for c in shares[2]:
            c.arrive()
        mid = pl.ds(HALO, depth)
        correction = part[it, own] + (part_in[it, 0, mid] + part_in[it, 1, mid])
        if it + 1 < ITERS:
            passing[0] = correction
            first = [
                between(low_lane, far_low, passing.at[0, depth - HALO :], passing.at[1, 0:HALO]),
                between(high_lane, far_high, passing.at[0, 0:HALO], passing.at[1, 0:HALO]),
            ]
            for c, a, b in ((first[0], far_low, high_lane), (first[1], far_high, low_lane)):
                c.arrive()
                across.append(between(a, b, passing.at[1, 0:HALO], beyond.at[1]))
        for c in edges:
            c.arrive()
        rest = jnp.zeros((depth - HALO, width), F32)
        correction = correction + jnp.concatenate([edge_in[it, 0], rest], axis=0)
        correction = correction + jnp.concatenate([rest, edge_in[it, 1]], axis=0)
        new = cur[it, own] * correction * (1.0 / views)
        if it + 1 < ITERS:
            cur[it + 1, own] = new
            for c in across:
                c.arrive()
            overlap = 2 * HALO - depth
            blank = jnp.zeros((depth - HALO, width), F32)
            for me, n, a in ((high_lane, 0, 0), (low_lane, 1, span - HALO)):

                @pl.when(l == me)
                def _(n=n, a=a, it=it):
                    got = beyond[0]
                    kept = (
                        jnp.concatenate([got[HALO - overlap :], blank], axis=0)
                        if n == 0
                        else jnp.concatenate([blank, got[:overlap]], axis=0)
                    )
                    total = edge[it, n] + (beyond[1] + kept)
                    rows_at = pl.ds(span + a, HALO)
                    cur[it + 1, rows_at] = cur[it, rows_at] * total * (1.0 / views)

            departed.extend(first + across)
        else:
            out[...] = new
        departed.extend(shares[0] + shares[1] + shares[2] + edges)
    for always, sent, c in routes:
        if always:
            c.wait_send()
        else:
            pl.when(sent)(c.wait_send)
    for c in departed + first_legs:
        c.leave()


def shards(groups, lanes, estimate, view_lines, line_owner, line_target, view_shift, psf_x, psf_yz):
    _, depth, width = estimate.shape
    views, n, _ = view_lines.shape
    cap = 2 * n // groups
    slots, span, all_rows = views * cap, depth + 2 * HALO, views * depth
    hbm = pl.BlockSpec(memory_space=pltpu.HBM)
    columns = -(-3 * span // 128) * 128
    plan, _ = relays(groups, lanes)
    copies = 18 * ITERS + 6 + len(plan)
    vmem = lambda *shape: pltpu.VMEM(shape, F32)
    dma = lambda n: pltpu.SemaphoreType.DMA((n,))
    out = pl.pallas_call(
        functools.partial(kernel, groups, lanes, views, cap),
        out_shape=jax.ShapeDtypeStruct((depth, width), F32),
        in_specs=[hbm] * 7,
        out_specs=pl.BlockSpec(memory_space=pltpu.VMEM),
        scratch_shapes=[
            vmem(views * n, width),
            pltpu.VMEM((views, n), jnp.int32),
            pltpu.VMEM((views, n), jnp.int32),
            pltpu.SMEM(view_shift.shape, jnp.int32),
            pltpu.SMEM(psf_x.shape, F32),
            pltpu.SMEM(psf_yz.shape, F32),
            dma(7),
            vmem(groups, slots, width),
            vmem(groups, slots, width),
            vmem(groups, 1, groups * slots),
            vmem(groups, 1, groups * slots),
            vmem(ITERS, columns, width),
            vmem(ITERS, columns, width),
            vmem(ITERS, 2, span, width),
            vmem(ITERS, 2, HALO, width),
            vmem(ITERS, 2, HALO, width),
            vmem(2, HALO, width),
            vmem(2, depth, width),
            vmem(len(plan), slots, width),
            pltpu.VMEM((2 * all_rows, columns), BF16),
            pltpu.VMEM((columns, 2 * all_rows), BF16),
            pltpu.VMEM((columns, all_rows), BF16),
            pltpu.VMEM((views, 256, 256), BF16),
            pltpu.VMEM((views, 256, 256), BF16),
            vmem(all_rows, width),
            vmem(all_rows, width),
            vmem(all_rows, width),
            dma(copies),
            dma(copies),
            dma(len(plan)),
            dma(groups),
            dma(groups),
            dma(groups),
            dma(groups),
        ],
        compiler_params=pltpu.CompilerParams(
            collective_id=0, has_side_effects=True, vmem_limit_bytes=64 << 20
        ),
    )(
        estimate.reshape(depth, width),
        view_lines.reshape(views * n, width),
        line_owner[:, :, 0],
        line_target,
        view_shift,
        psf_x,
        psf_yz,
    )
    return out.reshape(estimate.shape)


def solution(mesh):
    placed = (
        P("grp", "lane", None),
        P(None, ("grp", "lane"), None),
        P(None, ("grp", "lane"), None),
        P(None, ("grp", "lane")),
        P(),
        P(),
        P(),
    )
    return jax.shard_map(
        functools.partial(shards, mesh.shape["grp"], mesh.shape["lane"]),
        mesh=mesh, in_specs=placed, out_specs=P("grp", "lane", None), check_vma=False,
    )
```

```python
import functools

import jax
import jax.numpy as jnp
from jax import lax
from jax.experimental import pallas as pl
from jax.experimental.pallas import tpu as pltpu
from jax.sharding import PartitionSpec as P

ITERS = 2
CORNERS = 9
FAR_CORNERS = 12
AHEAD = 1
HALO = 24
MESH = pl.DeviceIdType.MESH
F32, BF16 = jnp.float32, jnp.bfloat16


def halves(x):
    high = x.astype(BF16)
    return high, (x - high.astype(F32)).astype(BF16)


def dot(a, b):
    return jnp.dot(a, b, preferred_element_type=F32)


def iota(shape, dim):
    return lax.broadcasted_iota(jnp.int32, shape, dim)


def total_of(ref, *at, size):
    summed = ref[(*at, 0)]
    for k in range(1, size):
        summed = summed + ref[(*at, k)]
    return summed


def along_y(x, taps):
    rows, width = x.shape
    blocks = width // 128
    padded = pltpu.roll(jnp.concatenate([x, jnp.zeros((rows, 128), F32)], axis=1), 64, 1)
    high, low = halves(padded)
    windows = [part[:, 128 * b : 128 * b + 256] for part in (high, low) for b in range(blocks)]
    r = dot(jnp.concatenate(windows, axis=0), taps)
    n = blocks * rows
    summed = r[:n, :128] + (r[:n, 128:] + r[n:, :128])
    return jnp.concatenate([summed[rows * b : rows * (b + 1)] for b in range(blocks)], axis=1)


def relays(groups, lanes):
    middle = groups // 2
    if lanes < 32 or groups < 8:
        return [(0, middle)], lanes // 2 - 1
    plan = [(0, middle+0), (0, middle-1), (0, middle+1), (0, middle+2), (1, middle+0)]
    return plan, lanes // 2 - 6


def kernel(groups, lanes, views, cap, est_at, lines_at, owner_at, target_at, shift_at, psf_x_at, psf_yz_at, out,
           lines, owners, targets, shift, psf_x, psf_yz, load_sem,
           outgoing, arrived, meta_out, meta_in, cur, part, part_in, edge, edge_in, beyond, passing, relayed,
           m_fwd, m_adj, m_adj_low, t_fwd, t_adj, observed, blurred, spread,
           send_sem, recv_sem, relay_send, a2a_send, a2a_recv, meta_send, meta_recv):
    p, l = lax.axis_index("grp"), lax.axis_index("lane")
    depth, width = est_at.shape
    taps = psf_yz.shape[2]
    reach = (taps - 1) // 2
    slots = views * cap
    span = depth + 2 * HALO
    all_rows = views * depth
    chunk = min(256, width)
    has = {"before": p > 0, "after": p < groups - 1, "up": l > 0, "down": l < lanes - 1}
    where = {
        "before": (jnp.maximum(p - 1, 0), l),
        "after": (jnp.minimum(p + 1, groups - 1), l),
        "up": (p, jnp.maximum(l - 1, 0)),
        "down": (p, jnp.minimum(l + 1, lanes - 1)),
    }
    opposite = {"before": "after", "after": "before", "up": "down", "down": "up"}
    counter = [0]

    class Copy:
        def __init__(self, to, since, target, src, dst, now=True):
            at = counter[0]
            counter[0] += 1
            self.to, self.since = to, since
            self.copy = pltpu.make_async_remote_copy(
                src_ref=src, dst_ref=dst, send_sem=send_sem.at[at], recv_sem=recv_sem.at[at],
                device_id=target, device_id_type=MESH,
            )
            if now:
                self.start()

        def start(self):
            pl.when(self.to)(self.copy.start)

        def arrive(self):
            pl.when(self.since)(self.copy.wait_recv)

        def leave(self):
            pl.when(self.to)(self.copy.wait_send)

    def beside(side, src, dst):
        return Copy(has[side], has[opposite[side]], where[side], src, dst)

    high_lane = lanes // 2
    low_lane = high_lane - 1
    far_low, far_high = high_lane - 4, high_lane + 3
    near = {"up": has["up"] & (l != high_lane), "down": has["down"] & (l != low_lane)}

    def between(a, b, src, dst, now=True):
        return Copy(l == a, l == b, (p, jnp.int32(b)), src, dst, now)

    half = lanes // 2
    from_end = jnp.minimum(l, lanes - 1 - l)
    plan, pool = relays(groups, lanes)

    def in_half(lane):
        return jnp.where(l < half, lane, lanes - 1 - lane)

    def relay_of(plane, n):
        return lax.rem(len(plan) * plane + n, pool)

    barrier = pltpu.get_barrier_semaphore()
    for k in range(1, groups):
        pl.semaphore_signal(barrier, inc=1, device_id=(lax.rem(p + k, groups), l), device_id_type=MESH)
    expected = groups - 1
    greeted = [(has[side], where[side]) for side in ("up", "down")]
    for a, b in ((far_low, low_lane), (far_low, high_lane), (low_lane - 1, high_lane),
                 (far_high, high_lane), (far_high, low_lane), (high_lane + 1, low_lane)):
        greeted += [(l == a, (p, jnp.int32(b))), (l == b, (p, jnp.int32(a)))]
    for cond, _ in greeted:
        expected = expected + jnp.where(cond, 1, 0)
    for n, (distance, k) in enumerate(plan):
        source = half - 1 - distance
        is_source, is_relay = from_end == source, from_end == relay_of(p, n)
        expected = expected + jnp.where(is_source, 1, 0) + jnp.where(is_relay, 1, 0)
        sender = lax.rem(p + groups - k, groups)
        greeted.append((is_relay, (p, in_half(source))))
        greeted.append((is_source, (sender, in_half(relay_of(sender, n)))))
    for cond, device in greeted:

        @pl.when(cond)
        def _(device=device):
            pl.semaphore_signal(barrier, inc=1, device_id=device, device_id_type=MESH)

    own = pl.ds(span + HALO, depth)
    loads = [
        pltpu.make_async_copy(src, dst, load_sem.at[n])
        for n, (src, dst) in enumerate((
            (owner_at, owners), (target_at, targets), (lines_at, lines), (est_at, cur.at[0, own]),
            (shift_at, shift), (psf_x_at, psf_x), (psf_yz_at, psf_yz),
        ))
    ]
    for c in loads:
        c.start()

    for it in range(ITERS):
        cur[it, 3 * span :] = jnp.zeros((cur.shape[1] - 3 * span, width), F32)

    @pl.when(p == 0)
    def _():
        for it in range(ITERS):
            cur[it, 0:span] = jnp.zeros((span, width), F32)
            part_in[it, 0] = jnp.zeros((span, width), F32)

    @pl.when(p == groups - 1)
    def _():
        for it in range(ITERS):
            cur[it, 2 * span : 3 * span] = jnp.zeros((span, width), F32)
            part_in[it, 1] = jnp.zeros((span, width), F32)

    @pl.when(l == 0)
    def _():
        for it in range(ITERS):
            cur[it, span : span + HALO] = jnp.zeros((HALO, width), F32)
            edge_in[it, 0] = jnp.zeros((HALO, width), F32)

    @pl.when(l == lanes - 1)
    def _():
        for it in range(ITERS):
            cur[it, 2 * span - HALO : 2 * span] = jnp.zeros((HALO, width), F32)
            edge_in[it, 1] = jnp.zeros((HALO, width), F32)

    for c in loads:
        c.wait()

    n_lines = lines.shape[0]
    per_view = n_lines // views
    owner = jnp.concatenate([owners[v : v + 1, :] for v in range(views)], axis=1)
    landing = jnp.concatenate([targets[v : v + 1, :] for v in range(views)], axis=1)
    line_at = iota((1, n_lines), 1)
    view = line_at // per_view
    key = view * groups + owner
    wide = jnp.broadcast_to(key, (n_lines, n_lines))
    earlier = iota((n_lines, n_lines), 0) < iota((n_lines, n_lines), 1)
    same = jnp.where((wide == wide.T) & earlier, 1.0, 0.0)
    rank = jnp.sum(same, axis=0, keepdims=True).astype(jnp.int32)
    in_block = view * cap + rank
    picks = jnp.where(iota((groups * slots, n_lines), 0) == owner * slots + in_block, 1.0, 0.0).astype(BF16)
    named = jnp.where(iota((groups, n_lines), 0) == owner, view * depth + landing + 1, 0)
    place = jnp.where(iota((groups * slots, n_lines), 0) == p * slots + in_block, 1.0, 0.0).astype(BF16)
    meta = lax.dot_general(
        named.astype(F32).astype(BF16), place, (((1,), (1,)), ((), ())), preferred_element_type=F32
    )
    for g in range(groups):
        meta_out[g] = meta[g : g + 1]
    picks2 = jnp.concatenate([picks, picks], axis=1)
    for at in range(0, width, chunk):
        high, low = halves(lines[:, at : at + chunk])
        packed = dot(picks2, jnp.concatenate([high, low], axis=0))
        outgoing[:, :, at : at + chunk] = packed.reshape(groups, slots, chunk)

    pl.semaphore_wait(barrier, expected)

    def widen_start(it):
        now = cur.at[it]
        lo, hi = span, 2 * span
        sides = near if it > 0 else has
        ups = [
            Copy(sides["up"], sides["down"], where["up"], now.at[lo + HALO : lo + 2 * HALO], now.at[hi - HALO : hi]),
            Copy(sides["down"], sides["up"], where["down"], now.at[hi - 2 * HALO : hi - HALO], now.at[lo : lo + HALO]),
        ]
        own_rows = now.at[lo + HALO : hi - HALO]
        mids = [
            beside("before", own_rows, now.at[2 * span + HALO : 3 * span - HALO]),
            beside("after", own_rows, now.at[HALO : span - HALO]),
        ]
        return ups, mids

    def widen_corners(it, ups, mids, who):
        now = cur.at[it]
        for c, at in ((ups[1], 0), (ups[0], span - HALO)):
            pl.when(who & c.since)(c.copy.wait_recv)
            got = now.at[span + at : span + at + HALO]
            for side, plane in (("before", 2), ("after", 0)):
                mids.append(Copy(
                    who & has[side], who & has[opposite[side]], where[side],
                    got, now.at[plane * span + at : plane * span + at + HALO],
                ))

    def widen_finish(ups, mids):
        for c in mids:
            c.arrive()
        departed.extend(ups + mids)

    departed = []
    first_legs = [
        Copy(
            from_end == half - 1 - distance, from_end == relay_of(p, n), (p, in_half(relay_of(p, n))),
            outgoing.at[lax.rem(p + k, groups)], relayed.at[n],
        )
        for n, (distance, k) in enumerate(plan)
    ]
    ups, mids = widen_start(0)
    routes = []

    def pass_on():
        for n, (distance, k) in enumerate(plan):
            first_legs[n].arrive()
            second = pltpu.make_async_remote_copy(
                src_ref=relayed.at[n], dst_ref=arrived.at[p], send_sem=relay_send.at[n], recv_sem=a2a_recv.at[k],
                device_id=(lax.rem(p + k, groups), in_half(half - 1 - distance)), device_id_type=MESH,
            )
            is_relay = from_end == relay_of(p, n)
            pl.when(is_relay)(second.start)
            routes.append((None, is_relay, second))

    order = sorted(range(1, groups), key=lambda k: -min(k, groups - k))
    for turn, k in enumerate(order):
        if turn == AHEAD % len(order):
            pass_on()
        if turn == CORNERS % len(order):
            widen_corners(0, ups, mids, from_end != half - 1)
        if turn == FAR_CORNERS % len(order):
            widen_corners(0, ups, mids, from_end == half - 1)
        to = (lax.rem(p + k, groups), l)
        direct = p >= 0
        for distance, offset in plan:
            if offset == k:
                direct = direct & (from_end != half - 1 - distance)
        for always, src, dst, sent, got in (
            (True, meta_out.at[to[0]], meta_in.at[p], meta_send, meta_recv),
            (False, outgoing.at[to[0]], arrived.at[p], a2a_send, a2a_recv),
        ):
            c = pltpu.make_async_remote_copy(
                src_ref=src, dst_ref=dst, send_sem=sent.at[k], recv_sem=got.at[k],
                device_id=to, device_id_type=MESH,
            )
            if always:
                c.start()
            else:
                pl.when(direct)(c.start)
            routes.append((always, direct, c))
    arrived[p] = outgoing[p]
    meta_in[p] = meta_out[p]

    columns = m_fwd.shape[1]
    column = iota((depth, columns), 1)
    plane = jnp.where(column < span, 0, jnp.where(column < 2 * span, 1, 2))
    tap_at = iota((depth, columns), 0) + (reach + HALO) - (column - plane * span)
    tap_at = jnp.where(column < 3 * span, tap_at, -1)
    blocks = []
    for v in range(views):
        acc = jnp.zeros((depth, columns), F32)
        for t in range(taps):
            acc = jnp.where(tap_at == t, psf_yz[v, 1, t], acc)
        across = jnp.where(plane == 0, psf_x[v, 2], jnp.where(plane == 1, psf_x[v, 1], psf_x[v, 0]))
        norm = jnp.full((1, columns), total_of(psf_yz, v, 1, size=taps)) * jnp.full(
            (1, columns), total_of(psf_x, v, size=3)
        )
        blocks.append(acc * across / norm)
    matrix = jnp.concatenate(blocks, axis=0)
    high, low = halves(matrix)
    m_fwd[0:all_rows] = high
    m_fwd[all_rows:] = low
    high, low = halves(matrix.T)
    m_adj[:, 0:all_rows] = high
    m_adj[:, all_rows:] = high
    m_adj_low[...] = low

    rows = 32

    def band(step, carry):
        i = iota((rows, 128), 0) + step * rows
        j = iota((rows, 128), 1)
        for v in range(views):
            norm = jnp.full((1, 128), total_of(psf_yz, v, 0, size=taps))
            for ref, at in ((t_fwd, j - i + (64 + reach + shift[v])), (t_adj, i - j + (reach - 64 + shift[v]))):
                acc = jnp.zeros((rows, 128), F32)
                for t in range(taps):
                    acc = jnp.where(at == t, psf_yz[v, 0, t], acc)
                high, low = halves(acc / norm)
                ref[v, pl.ds(pl.multiple_of(step * rows, rows), rows), 0:128] = high
                ref[v, pl.ds(pl.multiple_of(step * rows, rows), rows), 128:256] = low
        return carry

    lax.fori_loop(0, 256 // rows, band, 0)

    def blur(it):
        for at in range(0, width, chunk):
            high, low = halves(cur[it, :, at : at + chunk])
            r = dot(m_fwd[...], high)
            spread[:, at : at + chunk] = r[:all_rows] + (r[all_rows:] + dot(m_fwd[0:all_rows], low))
        for v in range(views):
            blurred[v * depth : (v + 1) * depth] = along_y(spread[v * depth : (v + 1) * depth], t_fwd[v])

    widen_finish(ups, mids)
    blur(0)

    first = [
        between(low_lane, far_low, passing.at[0, depth - HALO :], passing.at[1, 0:HALO], False),
        between(high_lane, far_high, passing.at[0, 0:HALO], passing.at[1, 0:HALO], False),
    ]
    across = []
    for c, a, b in ((first[0], far_low, high_lane), (first[1], far_high, low_lane)):
        c.arrive()
        across.append(between(a, b, passing.at[1, 0:HALO], beyond.at[1]))

    for always, sent, c in routes:
        if always is not None:
            c.wait_recv()
    marks = jnp.sum(meta_in[...], axis=0)
    lands = jnp.where(iota((all_rows, groups * slots), 0) + 1 == marks.astype(jnp.int32), 1.0, 0.0).astype(BF16)
    for at in range(0, width, chunk):
        high, low = halves(arrived[:, :, at : at + chunk].reshape(groups * slots, chunk))
        observed[:, at : at + chunk] = dot(lands, high) + dot(lands, low)

    for it in range(ITERS):
        if it > 0:
            ups, mids = widen_start(it)
            widen_corners(it, ups, mids, p >= 0)
            widen_finish(ups, mids)
            blur(it)
        y = iota((depth, width), 1)
        for v in range(views):
            at = pl.ds(v * depth, depth)
            seen = y + shift[v]
            quotient = jnp.where((seen >= 0) & (seen < width), observed[at] / blurred[at], 0.0)
            spread[at] = along_y(quotient, t_adj[v])
        for at in range(0, width, chunk):
            high, low = halves(spread[:, at : at + chunk])
            r = dot(m_adj[...], jnp.concatenate([high, low], axis=0)) + dot(m_adj_low[...], high)
            part[it, :, at : at + chunk] = r
        mine, theirs = part.at[it], part_in.at[it]
        shares = []
        for rows_at in ((0, HALO), (span - HALO, span), (HALO, span - HALO)):
            a, b = rows_at
            shares.append([
                beside("before", mine.at[a:b], theirs.at[1, a:b]),
                beside("after", mine.at[2 * span + a : 2 * span + b], theirs.at[0, a:b]),
            ])
        edges = []
        for n, (side, a) in enumerate((("up", 0), ("down", span - HALO))):
            for c in shares[n]:
                c.arrive()
            rows_at = pl.ds(a, HALO)
            edge[it, n] = part[it, pl.ds(span + a, HALO)] + (part_in[it, 0, rows_at] + part_in[it, 1, rows_at])
            edges.append(beside(side, edge.at[it, n], edge_in.at[it, 1 - n]))
        if it + 1 < ITERS:
            across += [
                between(low_lane - 1, high_lane, edge.at[it, 1], beyond.at[0]),
                between(high_lane + 1, low_lane, edge.at[it, 0], beyond.at[0]),
            ]
        for c in shares[2]:
            c.arrive()
        mid = pl.ds(HALO, depth)
        correction = part[it, own] + (part_in[it, 0, mid] + part_in[it, 1, mid])
        if it + 1 < ITERS:
            passing[0] = correction
            for c in first:
                c.start()
        for c in edges:
            c.arrive()
        rest = jnp.zeros((depth - HALO, width), F32)
        correction = correction + jnp.concatenate([edge_in[it, 0], rest], axis=0)
        correction = correction + jnp.concatenate([rest, edge_in[it, 1]], axis=0)
        new = cur[it, own] * correction * (1.0 / views)
        if it + 1 < ITERS:
            cur[it + 1, own] = new
            for c in across:
                c.arrive()
            overlap = 2 * HALO - depth
            blank = jnp.zeros((depth - HALO, width), F32)
            for me, n, a in ((high_lane, 0, 0), (low_lane, 1, span - HALO)):

                @pl.when(l == me)
                def _(n=n, a=a, it=it):
                    got = beyond[0]
                    kept = (
                        jnp.concatenate([got[HALO - overlap :], blank], axis=0)
                        if n == 0
                        else jnp.concatenate([blank, got[:overlap]], axis=0)
                    )
                    total = edge[it, n] + (beyond[1] + kept)
                    rows_at = pl.ds(span + a, HALO)
                    cur[it + 1, rows_at] = cur[it, rows_at] * total * (1.0 / views)

            departed.extend(first + across)
        else:
            out[...] = new
        departed.extend(shares[0] + shares[1] + shares[2] + edges)
    for always, sent, c in routes:
        if always:
            c.wait_send()
        else:
            pl.when(sent)(c.wait_send)
    for c in departed + first_legs:
        c.leave()


def shards(groups, lanes, estimate, view_lines, line_owner, line_target, view_shift, psf_x, psf_yz):
    _, depth, width = estimate.shape
    views, n, _ = view_lines.shape
    cap = 2 * n // groups
    slots, span, all_rows = views * cap, depth + 2 * HALO, views * depth
    hbm = pl.BlockSpec(memory_space=pltpu.HBM)
    columns = -(-3 * span // 128) * 128
    plan, _ = relays(groups, lanes)
    copies = 18 * ITERS + 10 + len(plan)
    vmem = lambda *shape: pltpu.VMEM(shape, F32)
    dma = lambda n: pltpu.SemaphoreType.DMA((n,))
    out = pl.pallas_call(
        functools.partial(kernel, groups, lanes, views, cap),
        out_shape=jax.ShapeDtypeStruct((depth, width), F32),
        in_specs=[hbm] * 7,
        out_specs=pl.BlockSpec(memory_space=pltpu.VMEM),
        scratch_shapes=[
            vmem(views * n, width),
            pltpu.VMEM((views, n), jnp.int32),
            pltpu.VMEM((views, n), jnp.int32),
            pltpu.SMEM(view_shift.shape, jnp.int32),
            pltpu.SMEM(psf_x.shape, F32),
            pltpu.SMEM(psf_yz.shape, F32),
            dma(7),
            vmem(groups, slots, width),
            vmem(groups, slots, width),
            vmem(groups, 1, groups * slots),
            vmem(groups, 1, groups * slots),
            vmem(ITERS, columns, width),
            vmem(ITERS, columns, width),
            vmem(ITERS, 2, span, width),
            vmem(ITERS, 2, HALO, width),
            vmem(ITERS, 2, HALO, width),
            vmem(2, HALO, width),
            vmem(2, depth, width),
            vmem(len(plan), slots, width),
            pltpu.VMEM((2 * all_rows, columns), BF16),
            pltpu.VMEM((columns, 2 * all_rows), BF16),
            pltpu.VMEM((columns, all_rows), BF16),
            pltpu.VMEM((views, 256, 256), BF16),
            pltpu.VMEM((views, 256, 256), BF16),
            vmem(all_rows, width),
            vmem(all_rows, width),
            vmem(all_rows, width),
            dma(copies),
            dma(copies),
            dma(len(plan)),
            dma(groups),
            dma(groups),
            dma(groups),
            dma(groups),
        ],
        compiler_params=pltpu.CompilerParams(
            collective_id=0, has_side_effects=True, vmem_limit_bytes=64 << 20
        ),
    )(
        estimate.reshape(depth, width),
        view_lines.reshape(views * n, width),
        line_owner[:, :, 0],
        line_target,
        view_shift,
        psf_x,
        psf_yz,
    )
    return out.reshape(estimate.shape)


def solution(mesh):
    placed = (
        P("grp", "lane", None),
        P(None, ("grp", "lane"), None),
        P(None, ("grp", "lane"), None),
        P(None, ("grp", "lane")),
        P(),
        P(),
        P(),
    )
    return jax.shard_map(
        functools.partial(shards, mesh.shape["grp"], mesh.shape["lane"]),
        mesh=mesh, in_specs=placed, out_specs=P("grp", "lane", None), check_vma=False,
    )
```

```python
import functools

import jax
import jax.numpy as jnp
from jax import lax
from jax.experimental import pallas as pl
from jax.experimental.pallas import tpu as pltpu
from jax.sharding import PartitionSpec as P

ITERS = 2
CORNERS = 3
FAR_CORNERS = 14
AHEAD = 1
HALO = 24
MESH = pl.DeviceIdType.MESH
F32, BF16 = jnp.float32, jnp.bfloat16


def halves(x):
    high = x.astype(BF16)
    return high, (x - high.astype(F32)).astype(BF16)


def dot(a, b):
    return jnp.dot(a, b, preferred_element_type=F32)


def iota(shape, dim):
    return lax.broadcasted_iota(jnp.int32, shape, dim)


def total_of(ref, *at, size):
    summed = ref[(*at, 0)]
    for k in range(1, size):
        summed = summed + ref[(*at, k)]
    return summed


def along_y(x, taps):
    rows, width = x.shape
    blocks = width // 128
    padded = pltpu.roll(jnp.concatenate([x, jnp.zeros((rows, 128), F32)], axis=1), 64, 1)
    high, low = halves(padded)
    windows = [part[:, 128 * b : 128 * b + 256] for part in (high, low) for b in range(blocks)]
    r = dot(jnp.concatenate(windows, axis=0), taps)
    n = blocks * rows
    summed = r[:n, :128] + (r[:n, 128:] + r[n:, :128])
    return jnp.concatenate([summed[rows * b : rows * (b + 1)] for b in range(blocks)], axis=1)


def relays(groups, lanes):
    middle = groups // 2
    if lanes < 32 or groups < 8:
        return [(0, middle)], lanes // 2 - 1
    plan = [(0, middle+0), (0, middle-1), (0, middle+1), (0, middle+2), (1, middle+0)]
    return plan, lanes // 2 - 6


def kernel(groups, lanes, views, cap, est_at, lines_at, owner_at, target_at, shift_at, psf_x_at, psf_yz_at, out,
           lines, owners, targets, shift, psf_x, psf_yz, load_sem,
           outgoing, arrived, meta_out, meta_in, cur, part, part_in, edge, edge_in, beyond, passing, relayed,
           m_fwd, m_adj, m_adj_low, t_fwd, t_adj, observed, blurred, spread,
           send_sem, recv_sem, relay_send, a2a_send, a2a_recv, meta_send, meta_recv):
    p, l = lax.axis_index("grp"), lax.axis_index("lane")
    depth, width = est_at.shape
    taps = psf_yz.shape[2]
    reach = (taps - 1) // 2
    slots = views * cap
    span = depth + 2 * HALO
    all_rows = views * depth
    chunk = min(256, width)
    has = {"before": p > 0, "after": p < groups - 1, "up": l > 0, "down": l < lanes - 1}
    where = {
        "before": (jnp.maximum(p - 1, 0), l),
        "after": (jnp.minimum(p + 1, groups - 1), l),
        "up": (p, jnp.maximum(l - 1, 0)),
        "down": (p, jnp.minimum(l + 1, lanes - 1)),
    }
    opposite = {"before": "after", "after": "before", "up": "down", "down": "up"}
    counter = [0]

    class Copy:
        def __init__(self, to, since, target, src, dst, now=True):
            at = counter[0]
            counter[0] += 1
            self.to, self.since = to, since
            self.copy = pltpu.make_async_remote_copy(
                src_ref=src, dst_ref=dst, send_sem=send_sem.at[at], recv_sem=recv_sem.at[at],
                device_id=target, device_id_type=MESH,
            )
            if now:
                self.start()

        def start(self):
            pl.when(self.to)(self.copy.start)

        def arrive(self):
            pl.when(self.since)(self.copy.wait_recv)

        def leave(self):
            pl.when(self.to)(self.copy.wait_send)

    def beside(side, src, dst):
        return Copy(has[side], has[opposite[side]], where[side], src, dst)

    high_lane = lanes // 2
    low_lane = high_lane - 1
    far_low, far_high = high_lane - 4, high_lane + 3
    near = {"up": has["up"] & (l != high_lane), "down": has["down"] & (l != low_lane)}

    def between(a, b, src, dst, now=True):
        return Copy(l == a, l == b, (p, jnp.int32(b)), src, dst, now)

    half = lanes // 2
    from_end = jnp.minimum(l, lanes - 1 - l)
    plan, pool = relays(groups, lanes)

    def in_half(lane):
        return jnp.where(l < half, lane, lanes - 1 - lane)

    def relay_of(plane, n):
        return lax.rem(len(plan) * plane + n, pool)

    barrier = pltpu.get_barrier_semaphore()
    for k in range(1, groups):
        pl.semaphore_signal(barrier, inc=1, device_id=(lax.rem(p + k, groups), l), device_id_type=MESH)
    expected = groups - 1
    greeted = [(has[side], where[side]) for side in ("up", "down")]
    for a, b in ((far_low, low_lane), (far_low, high_lane), (low_lane - 1, high_lane),
                 (far_high, high_lane), (far_high, low_lane), (high_lane + 1, low_lane)):
        greeted += [(l == a, (p, jnp.int32(b))), (l == b, (p, jnp.int32(a)))]
    for cond, _ in greeted:
        expected = expected + jnp.where(cond, 1, 0)
    for n, (distance, k) in enumerate(plan):
        source = half - 1 - distance
        is_source, is_relay = from_end == source, from_end == relay_of(p, n)
        expected = expected + jnp.where(is_source, 1, 0) + jnp.where(is_relay, 1, 0)
        sender = lax.rem(p + groups - k, groups)
        greeted.append((is_relay, (p, in_half(source))))
        greeted.append((is_source, (sender, in_half(relay_of(sender, n)))))
    for cond, device in greeted:

        @pl.when(cond)
        def _(device=device):
            pl.semaphore_signal(barrier, inc=1, device_id=device, device_id_type=MESH)

    own = pl.ds(span + HALO, depth)
    loads = [
        pltpu.make_async_copy(src, dst, load_sem.at[n])
        for n, (src, dst) in enumerate((
            (owner_at, owners), (target_at, targets), (lines_at, lines), (est_at, cur.at[0, own]),
            (shift_at, shift), (psf_x_at, psf_x), (psf_yz_at, psf_yz),
        ))
    ]
    for c in loads:
        c.start()

    for it in range(ITERS):
        cur[it, 3 * span :] = jnp.zeros((cur.shape[1] - 3 * span, width), F32)

    @pl.when(p == 0)
    def _():
        for it in range(ITERS):
            cur[it, 0:span] = jnp.zeros((span, width), F32)
            part_in[it, 0] = jnp.zeros((span, width), F32)

    @pl.when(p == groups - 1)
    def _():
        for it in range(ITERS):
            cur[it, 2 * span : 3 * span] = jnp.zeros((span, width), F32)
            part_in[it, 1] = jnp.zeros((span, width), F32)

    @pl.when(l == 0)
    def _():
        for it in range(ITERS):
            for plane in range(3) if it == 0 else (1,):
                cur[it, plane * span : plane * span + HALO] = jnp.zeros((HALO, width), F32)
            edge_in[it, 0] = jnp.zeros((HALO, width), F32)

    @pl.when(l == lanes - 1)
    def _():
        for it in range(ITERS):
            for plane in range(3) if it == 0 else (1,):
                cur[it, (plane + 1) * span - HALO : (plane + 1) * span] = jnp.zeros((HALO, width), F32)
            edge_in[it, 1] = jnp.zeros((HALO, width), F32)

    for c in loads:
        c.wait()

    n_lines = lines.shape[0]
    per_view = n_lines // views
    owner = jnp.concatenate([owners[v : v + 1, :] for v in range(views)], axis=1)
    landing = jnp.concatenate([targets[v : v + 1, :] for v in range(views)], axis=1)
    line_at = iota((1, n_lines), 1)
    view = line_at // per_view
    key = view * groups + owner
    wide = jnp.broadcast_to(key, (n_lines, n_lines))
    earlier = iota((n_lines, n_lines), 0) < iota((n_lines, n_lines), 1)
    same = jnp.where((wide == wide.T) & earlier, 1.0, 0.0)
    rank = jnp.sum(same, axis=0, keepdims=True).astype(jnp.int32)
    in_block = view * cap + rank
    picks = jnp.where(iota((groups * slots, n_lines), 0) == owner * slots + in_block, 1.0, 0.0).astype(BF16)
    named = jnp.where(iota((groups, n_lines), 0) == owner, view * depth + landing + 1, 0)
    place = jnp.where(iota((groups * slots, n_lines), 0) == p * slots + in_block, 1.0, 0.0).astype(BF16)
    meta = lax.dot_general(
        named.astype(F32).astype(BF16), place, (((1,), (1,)), ((), ())), preferred_element_type=F32
    )
    for g in range(groups):
        meta_out[g] = meta[g : g + 1]
    picks2 = jnp.concatenate([picks, picks], axis=1)
    for at in range(0, width, chunk):
        high, low = halves(lines[:, at : at + chunk])
        packed = dot(picks2, jnp.concatenate([high, low], axis=0))
        outgoing[:, :, at : at + chunk] = packed.reshape(groups, slots, chunk)

    pl.semaphore_wait(barrier, expected)

    def widen_start(it):
        now = cur.at[it]
        lo, hi = span, 2 * span
        sides = near if it > 0 else has
        ups = [
            Copy(sides["up"], sides["down"], where["up"], now.at[lo + HALO : lo + 2 * HALO], now.at[hi - HALO : hi]),
            Copy(sides["down"], sides["up"], where["down"], now.at[hi - 2 * HALO : hi - HALO], now.at[lo : lo + HALO]),
        ]
        own_rows = now.at[lo + HALO : hi - HALO]
        mids = [
            beside("before", own_rows, now.at[2 * span + HALO : 3 * span - HALO]),
            beside("after", own_rows, now.at[HALO : span - HALO]),
        ]
        return ups, mids

    def corners(it, c, at, who, mids):
        now = cur.at[it]
        pl.when(who & c.since)(c.copy.wait_recv)
        got = now.at[span + at : span + at + HALO]
        for side, plane in (("before", 2), ("after", 0)):
            mids.append(Copy(
                who & has[side], who & has[opposite[side]], where[side],
                got, now.at[plane * span + at : plane * span + at + HALO],
            ))

    def beside_planes(mids):
        now = cur.at[0]
        for c in mids:
            c.arrive()
        departed.extend(mids)
        mids.clear()
        for side, plane in (("before", 0), ("after", 2)):
            lo, hi = plane * span, (plane + 1) * span
            up, down = near["up"] & has[side], near["down"] & has[side]
            mids.append(Copy(up, down, where["up"], now.at[lo + HALO : lo + 2 * HALO], now.at[hi - HALO : hi]))
            mids.append(Copy(down, up, where["down"], now.at[hi - 2 * HALO : hi - HALO], now.at[lo : lo + HALO]))

    def widen_finish(ups, mids):
        for c in mids:
            c.arrive()
        departed.extend(ups + mids)

    departed = []
    first_legs = [
        Copy(
            from_end == half - 1 - distance, from_end == relay_of(p, n), (p, in_half(relay_of(p, n))),
            outgoing.at[lax.rem(p + k, groups)], relayed.at[n],
        )
        for n, (distance, k) in enumerate(plan)
    ]
    ups, mids = widen_start(0)
    routes = []

    def pass_on():
        for n, (distance, k) in enumerate(plan):
            first_legs[n].arrive()
            second = pltpu.make_async_remote_copy(
                src_ref=relayed.at[n], dst_ref=arrived.at[p], send_sem=relay_send.at[n], recv_sem=a2a_recv.at[k],
                device_id=(lax.rem(p + k, groups), in_half(half - 1 - distance)), device_id_type=MESH,
            )
            is_relay = from_end == relay_of(p, n)
            pl.when(is_relay)(second.start)
            routes.append((None, is_relay, second))

    order = sorted(range(1, groups), key=lambda k: -min(k, groups - k))
    for turn, k in enumerate(order):
        if turn == AHEAD % len(order):
            pass_on()
        if turn == CORNERS % len(order):
            beside_planes(mids)
        if turn == FAR_CORNERS % len(order):
            corners(0, ups[1], 0, l == high_lane, mids)
            corners(0, ups[0], span - HALO, l == low_lane, mids)
        to = (lax.rem(p + k, groups), l)
        direct = p >= 0
        for distance, offset in plan:
            if offset == k:
                direct = direct & (from_end != half - 1 - distance)
        for always, src, dst, sent, got in (
            (True, meta_out.at[to[0]], meta_in.at[p], meta_send, meta_recv),
            (False, outgoing.at[to[0]], arrived.at[p], a2a_send, a2a_recv),
        ):
            c = pltpu.make_async_remote_copy(
                src_ref=src, dst_ref=dst, send_sem=sent.at[k], recv_sem=got.at[k],
                device_id=to, device_id_type=MESH,
            )
            if always:
                c.start()
            else:
                pl.when(direct)(c.start)
            routes.append((always, direct, c))
    arrived[p] = outgoing[p]
    meta_in[p] = meta_out[p]

    columns = m_fwd.shape[1]
    column = iota((depth, columns), 1)
    plane = jnp.where(column < span, 0, jnp.where(column < 2 * span, 1, 2))
    tap_at = iota((depth, columns), 0) + (reach + HALO) - (column - plane * span)
    tap_at = jnp.where(column < 3 * span, tap_at, -1)
    blocks = []
    for v in range(views):
        acc = jnp.zeros((depth, columns), F32)
        for t in range(taps):
            acc = jnp.where(tap_at == t, psf_yz[v, 1, t], acc)
        across = jnp.where(plane == 0, psf_x[v, 2], jnp.where(plane == 1, psf_x[v, 1], psf_x[v, 0]))
        norm = jnp.full((1, columns), total_of(psf_yz, v, 1, size=taps)) * jnp.full(
            (1, columns), total_of(psf_x, v, size=3)
        )
        blocks.append(acc * across / norm)
    matrix = jnp.concatenate(blocks, axis=0)
    high, low = halves(matrix)
    m_fwd[0:all_rows] = high
    m_fwd[all_rows:] = low
    high, low = halves(matrix.T)
    m_adj[:, 0:all_rows] = high
    m_adj[:, all_rows:] = high
    m_adj_low[...] = low

    rows = 32

    def band(step, carry):
        i = iota((rows, 128), 0) + step * rows
        j = iota((rows, 128), 1)
        for v in range(views):
            norm = jnp.full((1, 128), total_of(psf_yz, v, 0, size=taps))
            for ref, at in ((t_fwd, j - i + (64 + reach + shift[v])), (t_adj, i - j + (reach - 64 + shift[v]))):
                acc = jnp.zeros((rows, 128), F32)
                for t in range(taps):
                    acc = jnp.where(at == t, psf_yz[v, 0, t], acc)
                high, low = halves(acc / norm)
                ref[v, pl.ds(pl.multiple_of(step * rows, rows), rows), 0:128] = high
                ref[v, pl.ds(pl.multiple_of(step * rows, rows), rows), 128:256] = low
        return carry

    lax.fori_loop(0, 256 // rows, band, 0)

    def blur(it):
        for at in range(0, width, chunk):
            high, low = halves(cur[it, :, at : at + chunk])
            r = dot(m_fwd[...], high)
            spread[:, at : at + chunk] = r[:all_rows] + (r[all_rows:] + dot(m_fwd[0:all_rows], low))
        for v in range(views):
            blurred[v * depth : (v + 1) * depth] = along_y(spread[v * depth : (v + 1) * depth], t_fwd[v])

    pl.when(ups[1].since & (l != high_lane))(ups[1].copy.wait_recv)
    pl.when(ups[0].since & (l != low_lane))(ups[0].copy.wait_recv)
    widen_finish(ups, mids)
    blur(0)

    first = [
        between(low_lane, far_low, passing.at[0, depth - HALO :], passing.at[1, 0:HALO], False),
        between(high_lane, far_high, passing.at[0, 0:HALO], passing.at[1, 0:HALO], False),
    ]
    across = []
    for c, a, b in ((first[0], far_low, high_lane), (first[1], far_high, low_lane)):
        c.arrive()
        across.append(between(a, b, passing.at[1, 0:HALO], beyond.at[1]))

    for always, sent, c in routes:
        if always is not None:
            c.wait_recv()
    marks = jnp.sum(meta_in[...], axis=0)
    lands = jnp.where(iota((all_rows, groups * slots), 0) + 1 == marks.astype(jnp.int32), 1.0, 0.0).astype(BF16)
    for at in range(0, width, chunk):
        high, low = halves(arrived[:, :, at : at + chunk].reshape(groups * slots, chunk))
        observed[:, at : at + chunk] = dot(lands, high) + dot(lands, low)

    for it in range(ITERS):
        if it > 0:
            ups, mids = widen_start(it)
            for c, at in ((ups[1], 0), (ups[0], span - HALO)):
                corners(it, c, at, p >= 0, mids)
            widen_finish(ups, mids)
            blur(it)
        y = iota((depth, width), 1)
        for v in range(views):
            at = pl.ds(v * depth, depth)
            seen = y + shift[v]
            quotient = jnp.where((seen >= 0) & (seen < width), observed[at] / blurred[at], 0.0)
            spread[at] = along_y(quotient, t_adj[v])
        for at in range(0, width, chunk):
            high, low = halves(spread[:, at : at + chunk])
            r = dot(m_adj[...], jnp.concatenate([high, low], axis=0)) + dot(m_adj_low[...], high)
            part[it, :, at : at + chunk] = r
        mine, theirs = part.at[it], part_in.at[it]
        shares = []
        for rows_at in ((0, HALO), (span - HALO, span), (HALO, span - HALO)):
            a, b = rows_at
            shares.append([
                beside("before", mine.at[a:b], theirs.at[1, a:b]),
                beside("after", mine.at[2 * span + a : 2 * span + b], theirs.at[0, a:b]),
            ])
        edges = []
        for n, (side, a) in enumerate((("up", 0), ("down", span - HALO))):
            for c in shares[n]:
                c.arrive()
            rows_at = pl.ds(a, HALO)
            edge[it, n] = part[it, pl.ds(span + a, HALO)] + (part_in[it, 0, rows_at] + part_in[it, 1, rows_at])
            edges.append(beside(side, edge.at[it, n], edge_in.at[it, 1 - n]))
        if it + 1 < ITERS:
            across += [
                between(low_lane - 1, high_lane, edge.at[it, 1], beyond.at[0]),
                between(high_lane + 1, low_lane, edge.at[it, 0], beyond.at[0]),
            ]
        for c in shares[2]:
            c.arrive()
        mid = pl.ds(HALO, depth)
        correction = part[it, own] + (part_in[it, 0, mid] + part_in[it, 1, mid])
        if it + 1 < ITERS:
            passing[0] = correction
            for c in first:
                c.start()
        for c in edges:
            c.arrive()
        rest = jnp.zeros((depth - HALO, width), F32)
        correction = correction + jnp.concatenate([edge_in[it, 0], rest], axis=0)
        correction = correction + jnp.concatenate([rest, edge_in[it, 1]], axis=0)
        new = cur[it, own] * correction * (1.0 / views)
        if it + 1 < ITERS:
            cur[it + 1, own] = new
            for c in across:
                c.arrive()
            overlap = 2 * HALO - depth
            blank = jnp.zeros((depth - HALO, width), F32)
            for me, n, a in ((high_lane, 0, 0), (low_lane, 1, span - HALO)):

                @pl.when(l == me)
                def _(n=n, a=a, it=it):
                    got = beyond[0]
                    kept = (
                        jnp.concatenate([got[HALO - overlap :], blank], axis=0)
                        if n == 0
                        else jnp.concatenate([blank, got[:overlap]], axis=0)
                    )
                    total = edge[it, n] + (beyond[1] + kept)
                    rows_at = pl.ds(span + a, HALO)
                    cur[it + 1, rows_at] = cur[it, rows_at] * total * (1.0 / views)

            departed.extend(first + across)
        else:
            out[...] = new
        departed.extend(shares[0] + shares[1] + shares[2] + edges)
    for always, sent, c in routes:
        if always:
            c.wait_send()
        else:
            pl.when(sent)(c.wait_send)
    for c in departed + first_legs:
        c.leave()


def shards(groups, lanes, estimate, view_lines, line_owner, line_target, view_shift, psf_x, psf_yz):
    _, depth, width = estimate.shape
    views, n, _ = view_lines.shape
    cap = 2 * n // groups
    slots, span, all_rows = views * cap, depth + 2 * HALO, views * depth
    hbm = pl.BlockSpec(memory_space=pltpu.HBM)
    columns = -(-3 * span // 128) * 128
    plan, _ = relays(groups, lanes)
    copies = 18 * ITERS + 14 + len(plan)
    vmem = lambda *shape: pltpu.VMEM(shape, F32)
    dma = lambda n: pltpu.SemaphoreType.DMA((n,))
    out = pl.pallas_call(
        functools.partial(kernel, groups, lanes, views, cap),
        out_shape=jax.ShapeDtypeStruct((depth, width), F32),
        in_specs=[hbm] * 7,
        out_specs=pl.BlockSpec(memory_space=pltpu.VMEM),
        scratch_shapes=[
            vmem(views * n, width),
            pltpu.VMEM((views, n), jnp.int32),
            pltpu.VMEM((views, n), jnp.int32),
            pltpu.SMEM(view_shift.shape, jnp.int32),
            pltpu.SMEM(psf_x.shape, F32),
            pltpu.SMEM(psf_yz.shape, F32),
            dma(7),
            vmem(groups, slots, width),
            vmem(groups, slots, width),
            vmem(groups, 1, groups * slots),
            vmem(groups, 1, groups * slots),
            vmem(ITERS, columns, width),
            vmem(ITERS, columns, width),
            vmem(ITERS, 2, span, width),
            vmem(ITERS, 2, HALO, width),
            vmem(ITERS, 2, HALO, width),
            vmem(2, HALO, width),
            vmem(2, depth, width),
            vmem(len(plan), slots, width),
            pltpu.VMEM((2 * all_rows, columns), BF16),
            pltpu.VMEM((columns, 2 * all_rows), BF16),
            pltpu.VMEM((columns, all_rows), BF16),
            pltpu.VMEM((views, 256, 256), BF16),
            pltpu.VMEM((views, 256, 256), BF16),
            vmem(all_rows, width),
            vmem(all_rows, width),
            vmem(all_rows, width),
            dma(copies),
            dma(copies),
            dma(len(plan)),
            dma(groups),
            dma(groups),
            dma(groups),
            dma(groups),
        ],
        compiler_params=pltpu.CompilerParams(
            collective_id=0, has_side_effects=True, vmem_limit_bytes=64 << 20
        ),
    )(
        estimate.reshape(depth, width),
        view_lines.reshape(views * n, width),
        line_owner[:, :, 0],
        line_target,
        view_shift,
        psf_x,
        psf_yz,
    )
    return out.reshape(estimate.shape)


def solution(mesh):
    placed = (
        P("grp", "lane", None),
        P(None, ("grp", "lane"), None),
        P(None, ("grp", "lane"), None),
        P(None, ("grp", "lane")),
        P(),
        P(),
        P(),
    )
    return jax.shard_map(
        functools.partial(shards, mesh.shape["grp"], mesh.shape["lane"]),
        mesh=mesh, in_specs=placed, out_specs=P("grp", "lane", None), check_vma=False,
    )
```
